256 devices in a mesh: grp: 8 (over y_lo, x), ctx: 32 (over z, y_hi, core).
Axes of the slice: x: 4, y: 4 (y_hi: 2, y_lo: 2; y = y_hi * 2 + y_lo), z: 8, core: 2. Of those that a mesh axis runs over, the one named last changes fastest.
Arguments:
- saved_mid: bfloat16 [32768, 1024], P(('grp', 'ctx')), parts along dimension 0, may hold values from -6 to 6
- upstream: bfloat16 [32768, 1024], P(('grp', 'ctx')), parts along dimension 0, may hold values from -6 to 6
- queries: bfloat16 [32768, 512], P(('grp', 'ctx')), parts along dimension 0
- keys_in: bfloat16 [32768, 512], P(('grp', 'ctx')), parts along dimension 0
- values_in: bfloat16 [32768, 512], P(('grp', 'ctx')), parts along dimension 0, may hold values from -6 to 6
- attn_out: bfloat16 [32768, 512], P(('grp', 'ctx')), parts along dimension 0, may hold values from -6 to 6
- log_norm: float32 [32768, 8], P(('grp', 'ctx')), parts along dimension 0, as said below
- out_proj: bfloat16 [512, 1024], replicated, may hold values from -0.1875 to 0.1875
- conv_weight: bfloat16 [31, 1024], replicated, may hold values from -2.5 to 2.5
- gates: float32 [32768, 2], P(('grp', 'ctx')), parts along dimension 0, may hold values from 0.1 to 0.9
- expert_ids: int32 [32768, 2], P(('grp', 'ctx')), parts along dimension 0, may hold values from 0 to 31, as said below
- slots: int32 [32768, 2], P(('grp', 'ctx')), parts along dimension 0, may hold values from 0 to 15, as said below
- w_in: bfloat16 [32, 1024, 2048], P('ctx'), may hold values from -0.1875 to 0.1875
- w_out: bfloat16 [32, 2048, 1024], P('ctx'), may hold values from -0.125 to 0.125
Outputs:
- d_mid: bfloat16 [32768, 1024], P(('grp', 'ctx')), parts along dimension 0
- d_queries: bfloat16 [32768, 512], P(('grp', 'ctx')), parts along dimension 0
- d_keys: bfloat16 [32768, 512], P(('grp', 'ctx')), parts along dimension 0
- d_values: bfloat16 [32768, 512], P(('grp', 'ctx')), parts along dimension 0
- d_conv: float32 [248, 1024], P('grp'), parts along dimension 0
- d_gates: bfloat16 [32768, 2], P(('grp', 'ctx')), parts along dimension 0
The draws below stay inside these ranges and needn't reach their ends.
There are 8 independent parts, one for each index of `grp`. The reference program is written for one: setup_inputs(seed, part) draws one part's arguments, and reference() takes and returns one part's arrays. A program takes and returns all parts, laid end to end along the dimension named above; an argument that names none is the same for every part. Nothing has to cross between parts.
Inputs may be any that keep to these rules, and one draw needn't show every extreme that they name: `expert_ids`: each frame names two different experts; within the frames of one block of 128, an expert is named at most 16 times. `slots`: within the frames of one block of 128, the (expert, slot) pairs are all different. log_norm[t, h] is the log of the sum over all 4096 frames u of exp(64 ** -0.5 queries_h[t] . keys_in_h[u]).
All inputs are finite; a program needn't handle non-finite values.
Results may differ from the reference program's by a relative error of at most 0.03.
Values may be sent and summed in bfloat16 or wider, within the bound.
A program may use at most 128 MiB of HBM per device.

```python
import jax
import jax.numpy as jnp
from jax import lax

D = 1024
HEADS = 8
HEAD_DIM = 64
EXP_HIDDEN = 2048
TAPS = 31
F_DEV = 128
HD = 512
FRAMES = 4096
EXPERTS = 32
CAP = 16
N_CTX = 32


def attention_pair(base_key):
    query_raw = jax.random.normal(jax.random.fold_in(base_key, 101), (FRAMES, HEADS * HEAD_DIM), jnp.float32) * 1.4
    key_raw = jax.random.normal(jax.random.fold_in(base_key, 102), (FRAMES, HEADS * HEAD_DIM), jnp.float32) * 1.4
    query_rows = query_raw.astype(jnp.bfloat16).astype(jnp.float32)
    key_rows = key_raw.astype(jnp.bfloat16).astype(jnp.float32)
    return (query_rows, key_rows)


def route_table(base_key):
    pool_size = EXPERTS * CAP
    blocks = FRAMES // F_DEV
    favored = jax.random.randint(jax.random.fold_in(base_key, 201), (), 0, EXPERTS)
    exponents = jax.random.randint(jax.random.fold_in(base_key, 202), (EXPERTS,), 4, 13)
    is_favored = jnp.arange(EXPERTS, dtype=jnp.int32) == favored
    highest = jnp.where(is_favored, 1, jnp.left_shift(1, exponents))
    lowest = jnp.where(is_favored, 0, 1)
    priority = jax.random.randint(jax.random.fold_in(base_key, 203), (blocks, EXPERTS, CAP), lowest[None, :, None], highest[None, :, None])
    combined = priority.reshape(blocks, pool_size) * pool_size + jnp.arange(pool_size, dtype=jnp.int32)[None, :]
    ranking = jnp.argsort(combined, axis=1)
    chosen = jnp.sort(ranking[:, :2 * F_DEV], axis=1)
    picked_experts = jnp.transpose((chosen // CAP).reshape(blocks, 2, F_DEV), (0, 2, 1))
    picked_slots = jnp.transpose((chosen % CAP).reshape(blocks, 2, F_DEV), (0, 2, 1))
    shuffle_scores = jax.random.randint(jax.random.fold_in(base_key, 204), (blocks, F_DEV), 0, 1 << 20) * F_DEV + jnp.arange(F_DEV, dtype=jnp.int32)[None, :]
    row_order = jnp.argsort(shuffle_scores, axis=1)
    picked_experts = jnp.take_along_axis(picked_experts, row_order[:, :, None], axis=1)
    picked_slots = jnp.take_along_axis(picked_slots, row_order[:, :, None], axis=1)
    return (picked_experts.reshape(FRAMES, 2).astype(jnp.int32), picked_slots.reshape(FRAMES, 2).astype(jnp.int32))


def draw_queries(key, part):
    query_rows, key_rows = attention_pair(key)
    return query_rows.astype(jnp.bfloat16)


def draw_keys_in(key, part):
    query_rows, key_rows = attention_pair(key)
    return key_rows.astype(jnp.bfloat16)


def draw_log_norm(key, part):
    query_rows, key_rows = attention_pair(key)
    query_heads = jnp.transpose(query_rows.reshape(FRAMES, HEADS, HEAD_DIM), (1, 0, 2))
    key_heads = jnp.transpose(key_rows.reshape(FRAMES, HEADS, HEAD_DIM), (1, 0, 2))

    def head_norm(head_pair):
        query_h, key_h = head_pair
        scores = jnp.dot(query_h, key_h.T, precision=lax.Precision.HIGHEST) * HEAD_DIM ** (-0.5)
        return jax.scipy.special.logsumexp(scores, axis=1)
    head_norms = lax.map(head_norm, (query_heads, key_heads))
    return jnp.transpose(head_norms).astype(jnp.float32)


def draw_expert_ids(key, part):
    picked_experts, picked_slots = route_table(key)
    return picked_experts


def draw_slots(key, part):
    picked_experts, picked_slots = route_table(key)
    return picked_slots


def block_levels(rng, shape, cuts, smallest, largest):
    def one(axis_at, parts):
        draws = jax.random.uniform(jax.random.fold_in(jax.random.fold_in(rng, 6), axis_at), (parts,), jnp.float32, smallest / len(cuts), largest / len(cuts))
        return jnp.repeat(jnp.exp(draws), shape[axis_at] // parts).reshape((-1,) + (1,) * (len(shape) - axis_at - 1))

    loudness = one(*cuts[0])
    for cut in cuts[1:]:
        loudness = loudness * one(*cut)
    return loudness


def centred(own_key, extent, scale, most, split=(), kind=jnp.bfloat16):
    values = jax.random.normal(own_key, extent, jnp.float32) * scale
    if len(split) > 0:
        values = block_levels(own_key, extent, split, -0.22, 0.18) * values
    return jnp.clip(values, min=-most, max=most).astype(kind)


def setup_inputs(seed: int = 0, part: int = 0) -> dict:
    key_list = jax.random.split(jax.random.key(seed), 15)
    part_splits = jax.random.split(jax.random.fold_in(key_list[14], part), 15)
    return {
        "saved_mid": centred(part_splits[0], (FRAMES, D), 1.0, 6.0, ((0, 32),)),
        "upstream": centred(part_splits[1], (FRAMES, D), 1.0, 6.0, ((0, 32),)),
        "queries": draw_queries(jax.random.fold_in(jax.random.fold_in(key_list[14], part), 71), part),
        "keys_in": draw_keys_in(jax.random.fold_in(jax.random.fold_in(key_list[14], part), 71), part),
        "values_in": centred(part_splits[4], (FRAMES, HD), 1.0, 6.0, ((0, 32),)),
        "attn_out": centred(part_splits[5], (FRAMES, HD), 1.0, 6.0, ((0, 32),)),
        "log_norm": draw_log_norm(jax.random.fold_in(jax.random.fold_in(key_list[14], part), 71), part),
        "out_proj": centred(key_list[7], (HD, D), D ** -0.5, 0.1875),
        "conv_weight": centred(key_list[8], (TAPS, D), 0.18, 2.5),
        "gates": jnp.clip(0.1 + 0.79999997 * jax.random.uniform(part_splits[9], (FRAMES, 2), jnp.float32) ** block_levels(part_splits[9], (FRAMES, 2), ((0, 32),), -0.2, 0.2), 0.1, 0.9),
        "expert_ids": draw_expert_ids(jax.random.fold_in(jax.random.fold_in(key_list[14], part), 71), part),
        "slots": draw_slots(jax.random.fold_in(jax.random.fold_in(key_list[14], part), 71), part),
        "w_in": centred(key_list[12], (EXPERTS, D, EXP_HIDDEN), D ** -0.5, 0.1875, ((0, 32),)),
        "w_out": centred(key_list[13], (EXPERTS, EXP_HIDDEN, D), EXP_HIDDEN ** -0.5, 0.125, ((0, 32),)),
    }


def expert_pass(operands):
    rows_in, rows_grad, w_input, w_output = operands
    hidden = jnp.dot(rows_in, w_input, preferred_element_type=jnp.float32)
    upward = lax.dot_general(rows_grad, w_output, (((1,), (1,)), ((), ())), preferred_element_type=jnp.float32)
    logistic = jax.nn.sigmoid(hidden)
    gate_unit = jnp.sum(hidden * logistic * upward, axis=1).astype(jnp.bfloat16)
    hidden_grad = (upward * logistic * (1.0 + hidden * (1.0 - logistic))).astype(jnp.bfloat16)
    input_grad = lax.dot_general(hidden_grad, w_input, (((1,), (1,)), ((), ())), preferred_element_type=jnp.float32)
    return input_grad.astype(jnp.bfloat16), gate_unit


def by_head(array):
    return jnp.transpose(array.reshape(FRAMES, HEADS, HEAD_DIM), (1, 0, 2))


def from_head(array):
    return jnp.transpose(array, (1, 0, 2)).reshape(FRAMES, HEADS * HEAD_DIM).astype(jnp.bfloat16)


def reference(saved_mid, upstream, queries, keys_in, values_in, attn_out, log_norm, out_proj, conv_weight, gates, expert_ids, slots, w_in, w_out):
    half_taps = (TAPS - 1) // 2
    weights = conv_weight.astype(jnp.float32)
    mid_float = saved_mid.astype(jnp.float32)
    mid_wide = jnp.pad(mid_float, ((half_taps, half_taps), (0, 0)))
    conv_total = jnp.zeros((FRAMES, D), jnp.float32)
    for offset in range(TAPS):
        conv_total = conv_total + weights[offset] * mid_wide[offset:offset + FRAMES]
    mixed_rows = (mid_float + conv_total).astype(jnp.bfloat16)
    source = (jnp.arange(FRAMES, dtype=jnp.int32) // F_DEV)[:, None]
    slot_total = EXPERTS * N_CTX * CAP
    flat_index = expert_ids * (N_CTX * CAP) + source * CAP + slots
    owner_row = jnp.full((slot_total,), FRAMES, jnp.int32).at[flat_index.reshape(-1)].set(
        jnp.repeat(jnp.arange(FRAMES, dtype=jnp.int32), 2))
    blank = jnp.zeros((1, D), jnp.bfloat16)
    rows_x = jnp.concatenate([mixed_rows, blank], 0)[owner_row].reshape(EXPERTS, N_CTX * CAP, D)
    rows_g = jnp.concatenate([upstream, blank], 0)[owner_row].reshape(EXPERTS, N_CTX * CAP, D)
    input_grad, gate_unit = lax.map(expert_pass, (rows_x, rows_g, w_in, w_out))
    picked = input_grad.reshape(slot_total, D)[flat_index]
    d_gates = gate_unit.reshape(slot_total)[flat_index]
    grad_sum = upstream.astype(jnp.float32) + gates[:, 0:1] * picked[:, 0].astype(jnp.float32)
    grad_sum = grad_sum + gates[:, 1:2] * picked[:, 1].astype(jnp.float32)
    grad_mixed = lax.optimization_barrier(grad_sum.astype(jnp.bfloat16))
    grad_float = grad_mixed.astype(jnp.float32)
    grad_wide = jnp.pad(grad_float, ((half_taps, half_taps), (0, 0)))
    dmid_total = grad_float
    for offset in range(TAPS):
        first_row = 2 * half_taps - offset
        dmid_total = dmid_total + weights[offset] * grad_wide[first_row:first_row + FRAMES]
    d_mid = dmid_total.astype(jnp.bfloat16)
    d_conv = jnp.stack([jnp.sum(mid_wide[offset:offset + FRAMES] * grad_float, axis=0) for offset in range(TAPS)])
    d_out = lax.dot_general(d_mid, out_proj, (((1,), (1,)), ((), ())), preferred_element_type=jnp.float32)
    d_out = lax.optimization_barrier(d_out.astype(jnp.bfloat16))
    row_delta = jnp.sum((d_out.astype(jnp.float32) * attn_out.astype(jnp.float32)).reshape(FRAMES, HEADS, HEAD_DIM), axis=2)
    score_scale = HEAD_DIM ** -0.5

    def head_pass(operands):
        query_h, key_h, value_h, dout_h, norm_h, delta_h = operands
        scores = jnp.dot(query_h, key_h.T, preferred_element_type=jnp.float32) * score_scale
        softmax_rows = jnp.exp(scores - norm_h[:, None])
        dprobs = jnp.dot(dout_h, value_h.T, preferred_element_type=jnp.float32)
        dscores = (softmax_rows * (dprobs - delta_h[:, None])).astype(jnp.bfloat16)
        query_grad = jnp.dot(dscores, key_h, preferred_element_type=jnp.float32) * score_scale
        key_grad = jnp.dot(dscores.T, query_h, preferred_element_type=jnp.float32) * score_scale
        value_grad = jnp.dot(softmax_rows.astype(jnp.bfloat16).T, dout_h, preferred_element_type=jnp.float32)
        return query_grad, key_grad, value_grad

    query_grad, key_grad, value_grad = lax.map(head_pass, (by_head(queries), by_head(keys_in), by_head(values_in), by_head(d_out), log_norm.T, row_delta.T))
    return d_mid, from_head(query_grad), from_head(key_grad), from_head(value_grad), d_conv, d_gates
```

```python
import jax
import jax.numpy as jnp
from jax import lax
from jax.experimental import pallas as pl
from jax.experimental.pallas import tpu as pltpu
from jax.sharding import PartitionSpec as P

MESH = pl.DeviceIdType.MESH
F32 = jnp.float32
BF16 = jnp.bfloat16

FR = 128
D = 1024
HEADS = 8
HID = 2048
TAPS = 31
CAP = 16
EXPERTS = 32
ROWS = EXPERTS * CAP
KEYS = 4096

S_G, S_X, S_R, S_T = 0, 32, 64, 96
S_HM, S_HG = 128, 130
S_Q, S_KV, S_KVP = 132, 140, 148
S_DO, S_DKVP, S_DKVZ, S_DQ = 152, 160, 164, 172
S_DC1, S_DC2, S_DC3 = 180, 188, 192
SEMS = 200

NT = (((1,), (1,)), ((), ()))


def dot(a, b):
    return jnp.dot(a, b, preferred_element_type=F32)


def dot_nt(a, b):
    return lax.dot_general(a, b, NT, preferred_element_type=F32)


def rem(a, b):
    return lax.rem(a, jnp.int32(b))


def div(a, b):
    return lax.div(a, jnp.int32(b))


def three_rows(rows, h):
    high = rows[h : h + 1, :].astype(BF16).astype(F32)
    rest = rows[h : h + 1, :] - high
    middle = rest.astype(BF16).astype(F32)
    low = rest - middle
    at = lax.broadcasted_iota(jnp.int32, (16, rows.shape[1]), 0)
    zero = jnp.zeros((16, rows.shape[1]), F32)
    block = jnp.where(at == 0, high, jnp.where(at == 1, middle, jnp.where(at == 2, low, zero)))
    return block.astype(BF16)


def lanes_below(shape, n):
    return lax.broadcasted_iota(jnp.int32, shape, 1) < n


def kernel(
    mid_ref, up_ref, q_ref, k_ref, v_ref, attn_ref, norm_ref, oproj_hbm, cw_ref, gates_ref, ids_ref,
    slots_ref, win_hbm, wout_hbm,
    dmid_ref, dq_ref, dk_ref, dv_ref, dconv_ref, dgates_ref,
    win, wout, oproj, wide, gwide, cwf, halo_m, halo_g, gm, pick, sg, sx, rg, rx, upw, hg, rs, rr,
    gs, gr, g2, qs, qr, ks, kva, qz, qn, nrow, kt, pt, dos, dor, doz, don, drow, attn_t, dkv_s, dkv_r,
    dkv0, dkv_z, dkv_o, dqa, dq_s, dq_o, dc_s, dc_r, dc1, dc2, dc3, dcf, tmp,
    ssem, rsem, wsem,
):
    grp, ctx = lax.axis_index("grp"), lax.axis_index("ctx")
    ylo, xx = div(grp, 4), rem(grp, 4)
    z, yhi, core = div(ctx, 4), rem(div(ctx, 2), 2), rem(ctx, 2)
    j = rem(ctx, 4)

    def near(dz, dj, in_group=False):
        dz, dj = jnp.int32(dz), jnp.int32(dj)
        dy, dc = div(dj, 2), rem(dj, 2)
        y_other = ylo if in_group else rem(ylo + dy, 2)
        return (
            y_other * 4 + xx,
            rem(z + dz, 8) * 4 + rem(yhi + dy, 2) * 2 + rem(core + dc, 2),
        )

    def along(step):
        return (grp, rem(ctx + step + 32, 32))

    def remote(src, dst, send_at, recv_at, device):
        return pltpu.make_async_remote_copy(
            src_ref=src, dst_ref=dst, send_sem=ssem.at[send_at], recv_sem=rsem.at[recv_at],
            device_id=device, device_id_type=MESH,
        )

    def arrived(ref, recv_at):
        remote(ref, ref, 0, recv_at, along(1)).wait_recv()

    def sent(ref, send_at):
        remote(ref, ref, send_at, 0, along(1)).wait_send()

    def place(k):
        n = div(k, 4)
        odd = rem(n, 2)
        return rem(odd * div(n + 1, 2) + (1 - odd) * (8 - div(n, 2)), 8), rem(k, 4)

    def slot_rows(k):
        return pl.ds(pl.multiple_of(k * CAP, CAP), CAP)

    w_copies = [
        pltpu.make_async_copy(wout_hbm.at[0], wout, wsem.at[0]),
        pltpu.make_async_copy(win_hbm.at[0], win, wsem.at[1]),
        pltpu.make_async_copy(oproj_hbm, oproj, wsem.at[2]),
    ]
    barrier = pltpu.get_barrier_semaphore()

    def greet(k, _):
        dz, dj = place(k)
        pl.semaphore_signal(barrier, inc=1, device_id=near(dz, dj), device_id_type=MESH)
        return 0

    lax.fori_loop(1, 32, greet, 0)
    for dj in (2, 3):
        pl.semaphore_signal(barrier, inc=1, device_id=near(0, dj, True), device_id_type=MESH)
    for step in (1, -1):
        pl.semaphore_signal(barrier, inc=1, device_id=along(step), device_id_type=MESH)
    for copy in w_copies:
        copy.start()

    ids, slot = ids_ref[...], slots_ref[...]
    planes_on = (jnp.right_shift(ids, 2) - z + 8) & 7
    in_plane = ((jnp.right_shift(ids, 1) + yhi) & 1) * 2 + ((ids + core) & 1)
    spot = planes_on * 4 + in_plane
    sid = spot * CAP + slot
    lane = lax.broadcasted_iota(jnp.int32, (FR, ROWS), 1)
    both = jnp.zeros((FR, ROWS), F32)
    for r in range(2):
        hit = jnp.where(lane == sid[:, r : r + 1], 1.0, 0.0).astype(F32)
        pick[r] = hit.astype(BF16)
        both = both + hit
    spread = jnp.transpose(both).astype(BF16)

    for n in range(4):
        rows = slice(n * 128, n * 128 + 128)
        sg[rows, :] = dot(spread[rows, :], up_ref[...]).astype(BF16)
    rg[0:CAP, :] = sg[0:CAP, :]

    pl.semaphore_wait(barrier, 35)

    halo_m_out = [
        remote(mid_ref.at[pl.ds(FR - 16, 16)], halo_m.at[0], S_HM, S_HM, along(1)),
        remote(mid_ref.at[pl.ds(0, 16)], halo_m.at[1], S_HM + 1, S_HM + 1, along(-1)),
    ]
    for copy in halo_m_out:
        copy.start()

    def spread_out(src, dst, first):
        def body(k, _):
            dz, dj = place(k)
            here = dz * 4 + dj
            there = rem(8 - dz, 8) * 4 + dj
            remote(
                src.at[slot_rows(here)], dst.at[slot_rows(there)], first + here, first + there, near(dz, dj)
            ).start()
            return 0

        lax.fori_loop(1, 32, body, 0)

    spread_out(sg, rg, S_G)

    cwf[0:TAPS, :] = cw_ref[...].astype(F32)
    tmp[...] = jnp.zeros((FR, 128), F32)
    tmp[:, 0:HEADS] = norm_ref[...]
    norm_t = jnp.transpose(tmp[...])
    for n in range(4):
        cols = slice(n * 128, n * 128 + 128)
        q_t = jnp.transpose(q_ref[:, cols].astype(F32) * 0.125).astype(BF16)
        attn_t[cols, :] = jnp.transpose(attn_ref[:, cols].astype(F32))
        kk, vv = k_ref[:, cols].astype(F32), v_ref[:, cols].astype(F32)
        first = lanes_below((FR, 128), 64)
        ks[2 * n] = jnp.where(first, kk, pltpu.roll(vv, 64, 1)).astype(BF16)
        ks[2 * n + 1] = jnp.where(first, pltpu.roll(kk, 64, 1), vv).astype(BF16)
        for half in range(2):
            h = 2 * n + half
            qs[h * 80 : h * 80 + 64, :] = q_t[half * 64 : half * 64 + 64, :]
            qs[h * 80 + 64 : h * 80 + 80, :] = three_rows(norm_t, h)

    def head_rows(h):
        return pl.ds(pl.multiple_of(h * 80, 16), 80)

    wide[16 : 16 + FR, :] = mid_ref[...].astype(F32)
    for side, copy in enumerate(halo_m_out):
        arrived(halo_m.at[side], S_HM + side)
    not_first = jnp.where(ctx > 0, 1.0, 0.0).astype(F32)
    not_last = jnp.where(ctx < 31, 1.0, 0.0).astype(F32)
    wide[0:16, :] = halo_m[0].astype(F32) * not_first
    wide[16 + FR : 32 + FR, :] = halo_m[1].astype(F32) * not_last

    def lane_tile(i):
        return pl.ds(pl.multiple_of(i * 128, 128), 128)

    def convolve(src, dst, backward):
        def body(i, _):
            cols = lane_tile(i)
            total = src[pl.ds(16, FR), cols]
            for o in range(1, TAPS + 1):
                tap = TAPS - o if backward else o - 1
                total = total + cwf[pl.ds(tap, 1), cols] * src[pl.ds(o, FR), cols]
            dst[:, cols] = total.astype(BF16)
            return 0

        lax.fori_loop(0, 8, body, 0)

    convolve(wide, gm, False)
    for n in range(4):
        rows = slice(n * 128, n * 128 + 128)
        sx[rows, :] = dot(spread[rows, :], gm[...]).astype(BF16)
    rx[0:CAP, :] = sx[0:CAP, :]
    spread_out(sx, rx, S_X)

    w_copies[0].wait()
    w_copies[1].wait()

    def g_arrived(k, _):
        arrived(rg.at[slot_rows(k)], S_G + k)
        return 0

    lax.fori_loop(1, 32, g_arrived, 0)

    def upward_tile(i, _):
        rows = pl.ds(pl.multiple_of(i * 256, 256), 256)
        upw[:, rows] = dot_nt(rg[...], wout[rows, :])
        return 0

    lax.fori_loop(0, HID // 256, upward_tile, 0)

    for chunk in (0, 3, 1, 2):
        rows = slice(chunk * 128, chunk * 128 + 128)

        def x_arrived(k, _):
            arrived(rx.at[slot_rows(k)], S_X + k)
            return 0

        lax.fori_loop(max(chunk * 8, 1), chunk * 8 + 8, x_arrived, 0)

        def hidden_tile(i, gate):
            cols = pl.ds(pl.multiple_of(i * 256, 256), 256)
            pre = dot(rx[rows, :], win[:, cols])
            upward = upw[rows, cols]
            sig = jax.nn.sigmoid(pre)
            unit = pre * sig * upward
            hg[:, cols] = (upward * sig * (1.0 + pre * (1.0 - sig))).astype(BF16)
            return gate + unit[:, 0:128] + unit[:, 128:256]

        gate = lax.fori_loop(0, HID // 256, hidden_tile, jnp.zeros((FR, 128), F32))
        gate_row = jnp.sum(jnp.transpose(gate), axis=0, keepdims=True).astype(BF16).astype(F32)
        gs[chunk] = gate_row

        def grad_tile(i, _):
            cols = pl.ds(pl.multiple_of(i * 256, 256), 256)
            rs[rows, cols] = dot_nt(hg[...], win[cols, :]).astype(BF16)
            return 0

        lax.fori_loop(0, D // 256, grad_tile, 0)

        def give_back(k, _):
            dz, dj = div(k, 4), rem(k, 4)
            there = rem(8 - dz, 8) * 4 + dj
            device = near(dz, dj)
            remote(rs.at[slot_rows(k)], rr.at[slot_rows(there)], S_R + k, S_R + there, device).start()
            remote(gs.at[chunk], gr.at[there], S_T + k, S_T + there, device).start()
            return 0

        lax.fori_loop(max(chunk * 8, 1), chunk * 8 + 8, give_back, 0)
    rr[0:CAP, :] = rs[0:CAP, :]
    gr[0] = gs[0]

    qr[0] = qs[head_rows(z), :]
    kva[0:FR, :] = ks[z]

    def to_planes(dz, _):
        h = rem(z + dz, 8)
        back = 8 - dz
        device = near(dz, 0)
        remote(qs.at[head_rows(h)], qr.at[back], S_Q + dz, S_Q + back, device).start()
        remote(
            ks.at[h], kva.at[pl.ds(pl.multiple_of(back * FR, FR), FR)], S_KV + dz, S_KV + back, device
        ).start()
        return 0

    lax.fori_loop(1, 8, to_planes, 0)

    def r_arrived(k, _):
        arrived(rr.at[slot_rows(k)], S_R + k)
        return 0

    lax.fori_loop(1, 32, r_arrived, 0)
    gates = gates_ref[...]
    for n in range(4):
        cols = slice(n * 256, n * 256 + 256)
        back = rr[:, cols]
        grad = up_ref[:, cols].astype(F32)
        grad = grad + gates[:, 0:1] * dot(pick[0], back)
        grad = grad + gates[:, 1:2] * dot(pick[1], back)
        gm[:, cols] = grad.astype(BF16)

    halo_g_out = [
        remote(gm.at[pl.ds(FR - 16, 16)], halo_g.at[0], S_HG, S_HG, along(1)),
        remote(gm.at[pl.ds(0, 16)], halo_g.at[1], S_HG + 1, S_HG + 1, along(-1)),
    ]
    for copy in halo_g_out:
        copy.start()
    gwide[16 : 16 + FR, :] = gm[...].astype(F32)

    def kv_arrived(k, _):
        arrived(kva.at[pl.ds(pl.multiple_of(k * FR, FR), FR)], S_KV + k)
        return 0

    lax.fori_loop(1, 8, kv_arrived, 0)
    for dj in (2, 3, 1):
        remote(
            kva.at[pl.ds(0, 1024)], kva.at[pl.ds(dj * 1024, 1024)], S_KVP + dj, S_KVP + dj, near(0, dj, True)
        ).start()

    def tap_tile(i, _):
        cols = lane_tile(i)
        here = gwide[pl.ds(16, FR), cols]
        for o in range(1, TAPS + 1):
            part = jnp.sum((wide[pl.ds(o, FR), cols] * here).reshape(16, 8, 128), axis=0)
            dc_s[i, pl.ds(o - 1, 1), :] = jnp.sum(part, axis=0, keepdims=True)
        dc_s[i, pl.ds(TAPS, 1), :] = jnp.zeros((1, 128), F32)
        return 0

    lax.fori_loop(0, 8, tap_tile, 0)

    def taps_out(dz, _):
        remote(dc_s.at[rem(z + dz, 8)], dc_r.at[8 - dz], S_DC1 + dz, S_DC1 + 8 - dz, near(dz, 0)).start()
        return 0

    for side in range(2):
        arrived(halo_g.at[side], S_HG + side)
    gwide[0:16, :] = halo_g[0].astype(F32) * not_first
    gwide[16 + FR : 32 + FR, :] = halo_g[1].astype(F32) * not_last
    convolve(gwide, dmid_ref, True)

    w_copies[2].wait()
    grad_out = dot_nt(oproj[...], dmid_ref[...]).astype(BF16)
    delta = jnp.sum((grad_out.astype(F32) * attn_t[...]).reshape(HEADS, 64, FR), axis=1)
    for h in range(HEADS):
        dos[h * 80 : h * 80 + 64, :] = grad_out[h * 64 : h * 64 + 64, :]
        dos[h * 80 + 64 : h * 80 + 80, :] = three_rows(delta, h)
    dor[0] = dos[head_rows(z), :]

    def dout_to_planes(dz, _):
        back = 8 - dz
        remote(dos.at[head_rows(rem(z + dz, 8))], dor.at[back], S_DO + dz, S_DO + back, near(dz, 0)).start()
        return 0

    lax.fori_loop(1, 8, dout_to_planes, 0)
    lax.fori_loop(1, 8, taps_out, 0)

    def q_arrived(k, _):
        arrived(qr.at[k], S_Q + k)
        return 0

    lax.fori_loop(1, 8, q_arrived, 0)
    qz[64:128, :] = jnp.zeros((64, 1024), BF16)
    for b in range(8):
        cols = slice(b * 128, b * 128 + 128)
        qz[0:64, cols] = qr[b, 0:64, :]
        nrow[:, cols] = jnp.sum(qr[b, 64:80, :].astype(F32), axis=0, keepdims=True)
        qn[cols, :] = jnp.transpose(qz[:, cols].astype(F32)).astype(BF16)
    for dj in (1, 2, 3):
        arrived(kva.at[pl.ds(dj * 1024, 1024)], S_KVP + dj)

    def prob_tile(i, _):
        rows = pl.ds(pl.multiple_of(i * 256, 256), 256)
        tile = kva[rows, :]
        kt[:, rows] = jnp.transpose(tile.astype(F32))[0:64, :].astype(BF16)
        pt[rows, :] = jnp.exp(dot(tile, qz[...]) - nrow[...]).astype(BF16)
        return 0

    lax.fori_loop(0, KEYS // 256, prob_tile, 0)

    def do_arrived(k, _):
        arrived(dor.at[k], S_DO + k)
        return 0

    lax.fori_loop(1, 8, do_arrived, 0)
    doz[0:64, :] = jnp.zeros((64, 1024), BF16)
    for b in range(8):
        cols = slice(b * 128, b * 128 + 128)
        doz[64:128, cols] = dor[b, 0:64, :]
        drow[:, cols] = jnp.sum(dor[b, 64:80, :].astype(F32), axis=0, keepdims=True)
        don[cols, :] = jnp.transpose(doz[:, cols].astype(F32)).astype(BF16)
    dqa[...] = jnp.zeros((64, 1024), F32)

    for dj in (3, 2, 1, 0):

        def score_tile(i, _):
            at = pl.multiple_of(i * 256, 256)
            rows = pl.ds(pl.multiple_of(dj * 1024 + at, 256), 256)
            prob = pt[rows, :]
            dprob = dot(kva[rows, :], doz[...]) - drow[...]
            score = (prob.astype(F32) * dprob).astype(BF16)
            both_grads = dot(score, qn[...]) + dot(prob, don[...])
            if dj:
                dkv_s[dj - 1, pl.ds(at, 256), :] = both_grads.astype(BF16)
            else:
                dkv0[pl.ds(at, 256), :] = both_grads
            dqa[...] += dot(kt[:, rows], score)
            return 0

        lax.fori_loop(0, 4, score_tile, 0)
        if dj:
            remote(
                dkv_s.at[dj - 1], dkv_r.at[dj - 1], S_DKVP + dj, S_DKVP + dj, near(0, dj, True)
            ).start()

    for b in range(8):
        dq_s[b] = (dqa[:, b * 128 : b * 128 + 128] * 0.125).astype(BF16)
    z_rows = pl.ds(pl.multiple_of(z * 64, 64), 64)
    dq_o[z_rows, :] = dq_s[0]

    def dq_home(dz, _):
        remote(dq_s.at[dz], dq_o.at[z_rows], S_DQ + dz, S_DQ + 8 - dz, near(dz, 0)).start()
        return 0

    lax.fori_loop(1, 8, dq_home, 0)

    def dc1_arrived(k, _):
        arrived(dc_r.at[k], S_DC1 + k)
        return 0

    lax.fori_loop(1, 8, dc1_arrived, 0)
    taps = dc_s[z]
    for b in range(1, 8):
        taps = taps + dc_r[b]
    dc1[...] = taps
    dc2[j] = taps
    for dj in (2, 3, 1):
        remote(dc1, dc2.at[j], S_DC2 + dj, S_DC2 + dj, near(0, dj, True)).start()

    for dj in (3, 2, 1):
        arrived(dkv_r.at[dj - 1], S_DKVP + dj)

    def sum_keys(k, _):
        n = rem(k + 1, 8)
        rows = pl.ds(pl.multiple_of(n * FR, FR), FR)
        total = dkv0[rows, :]
        for p in range(3):
            total = total + dkv_r[p, rows, :].astype(F32)
        dkv_z[n] = total.astype(BF16)

        @pl.when(n > 0)
        def _():
            remote(dkv_z.at[n], dkv_o.at[z], S_DKVZ + n, S_DKVZ + rem(8 - n, 8), near(n, 0)).start()

        return 0

    lax.fori_loop(0, 8, sum_keys, 0)
    dkv_o[z] = dkv_z[0]

    for dj in (1, 2, 3):
        arrived(dc1, S_DC2 + dj)
    dc3[...] = (dc2[0] + dc2[1]) + (dc2[2] + dc2[3])
    dcf[z] = dc3[...]

    def taps_home(dz, _):
        remote(dc3, dcf.at[z], S_DC3 + dz, S_DC3 + 8 - dz, near(dz, 0)).start()
        return 0

    lax.fori_loop(1, 8, taps_home, 0)

    def t_arrived(k, _):
        arrived(gr.at[k], S_T + k)
        return 0

    lax.fori_loop(1, 32, t_arrived, 0)
    for k in range(EXPERTS):
        g2[k : k + 1, :] = gr[k]
    spot_lane = lax.broadcasted_iota(jnp.int32, (FR, EXPERTS), 1)
    lane_128 = lax.broadcasted_iota(jnp.int32, (FR, 128), 1)
    units = g2[...].astype(BF16)
    for r in range(2):
        of_spot = jnp.where(spot_lane == spot[:, r : r + 1], 1.0, 0.0).astype(BF16)
        line = dot(of_spot, units)
        own = lane_128 == (sid[:, r : r + 1] & 127)
        dgates_ref[:, r : r + 1] = jnp.sum(jnp.where(own, line, 0.0), axis=1, keepdims=True).astype(BF16)

    def dq_arrived(k, _):
        arrived(dq_s.at[k], S_DQ + k)
        return 0

    lax.fori_loop(1, 8, dq_arrived, 0)
    for n in range(4):
        cols = slice(n * 128, n * 128 + 128)
        dq_ref[:, cols] = jnp.transpose(dq_o[cols, :].astype(F32)).astype(BF16)

    def dkv_arrived(k, _):
        arrived(dkv_z.at[k], S_DKVZ + k)
        return 0

    lax.fori_loop(1, 8, dkv_arrived, 0)
    for n in range(4):
        cols = slice(n * 128, n * 128 + 128)
        first = lanes_below((FR, 128), 64)
        one, two = dkv_o[2 * n].astype(F32), dkv_o[2 * n + 1].astype(F32)
        dk_ref[:, cols] = jnp.where(first, one, pltpu.roll(two, 64, 1)).astype(BF16)
        dv_ref[:, cols] = jnp.where(first, pltpu.roll(one, 64, 1), two).astype(BF16)

    def dc3_arrived(k, _):
        arrived(dc3, S_DC3 + k)
        return 0

    lax.fori_loop(1, 8, dc3_arrived, 0)
    for n in range(8):
        dconv_ref[:, n * 128 : n * 128 + 128] = dcf[n, 0:TAPS, :]

    def rows_left(k, _):
        for first in (S_G, S_X, S_R):
            sent(sg.at[slot_rows(k)], first + k)
        sent(gr.at[k], S_T + k)
        return 0

    lax.fori_loop(1, 32, rows_left, 0)

    def blocks_left(k, _):
        sent(qr.at[k], S_Q + k)
        sent(ks.at[k], S_KV + k)
        sent(dor.at[k], S_DO + k)
        sent(dkv_z.at[k], S_DKVZ + k)
        sent(dq_s.at[k], S_DQ + k)
        sent(dc_r.at[k], S_DC1 + k)
        sent(dc3, S_DC3 + k)
        return 0

    lax.fori_loop(1, 8, blocks_left, 0)
    for copy in halo_m_out + halo_g_out:
        copy.wait_send()
    for dj in (1, 2, 3):
        sent(kva.at[pl.ds(0, 1024)], S_KVP + dj)
        sent(dkv_s.at[dj - 1], S_DKVP + dj)
        sent(dc1, S_DC2 + dj)


def on_device(*args):
    vmem, anywhere = pl.BlockSpec(memory_space=pltpu.VMEM), pl.BlockSpec(memory_space=pl.ANY)
    in_specs = [vmem] * 14
    for n in (7, 12, 13):
        in_specs[n] = anywhere
    V = pltpu.VMEM
    scratch = [
        V((D, HID), BF16), V((HID, D), BF16), V((512, D), BF16),
        V((160, D), F32), V((160, D), F32), V((32, D), F32),
        V((2, 16, D), BF16), V((2, 16, D), BF16), V((FR, D), BF16), V((2, FR, ROWS), BF16),
        V((ROWS, D), BF16), V((ROWS, D), BF16), V((ROWS, D), BF16), V((ROWS, D), BF16),
        V((ROWS, HID), F32), V((FR, HID), BF16), V((ROWS, D), BF16), V((ROWS, D), BF16),
        V((4, 1, 128), F32), V((EXPERTS, 1, 128), F32), V((EXPERTS, 128), F32),
        V((640, 128), BF16), V((8, 80, 128), BF16), V((8, FR, 128), BF16), V((KEYS, 128), BF16),
        V((128, 1024), BF16), V((1024, 128), BF16), V((1, 1024), F32), V((64, KEYS), BF16), V((KEYS, 1024), BF16),
        V((640, 128), BF16), V((8, 80, 128), BF16), V((128, 1024), BF16), V((1024, 128), BF16), V((1, 1024), F32),
        V((512, FR), F32), V((3, 1024, 128), BF16), V((3, 1024, 128), BF16),
        V((1024, 128), F32), V((8, FR, 128), BF16), V((8, FR, 128), BF16),
        V((64, 1024), F32), V((8, 64, 128), BF16), V((512, 128), BF16),
        V((8, 32, 128), F32), V((8, 32, 128), F32), V((32, 128), F32), V((4, 32, 128), F32), V((32, 128), F32),
        V((8, 32, 128), F32), V((FR, 128), F32),
        pltpu.SemaphoreType.DMA((SEMS,)), pltpu.SemaphoreType.DMA((SEMS,)), pltpu.SemaphoreType.DMA((3,)),
    ]
    shape = jax.ShapeDtypeStruct
    return pl.pallas_call(
        kernel,
        out_shape=(
            shape((FR, D), BF16), shape((FR, 512), BF16), shape((FR, 512), BF16), shape((FR, 512), BF16),
            shape((TAPS, D), F32), shape((FR, 2), BF16),
        ),
        in_specs=in_specs,
        out_specs=(vmem,) * 6,
        scratch_shapes=scratch,
        compiler_params=pltpu.CompilerParams(
            collective_id=0, has_side_effects=True, vmem_limit_bytes=58 * 1024 * 1024
        ),
        name="conformer_backward",
    )(*args)


def solution(mesh):
    frames = P(("grp", "ctx"), None)
    in_specs = (frames,) * 7 + (P(), P()) + (frames,) * 3 + (P("ctx", None, None),) * 2
    out_specs = (frames,) * 4 + (P("grp", None), frames)
    return jax.shard_map(on_device, mesh=mesh, in_specs=in_specs, out_specs=out_specs, check_vma=False)
```

```python
import jax
import jax.numpy as jnp
from jax import lax
from jax.experimental import pallas as pl
from jax.experimental.pallas import tpu as pltpu
from jax.sharding import PartitionSpec as P

MESH = pl.DeviceIdType.MESH
F32 = jnp.float32
BF16 = jnp.bfloat16

FR = 128
D = 1024
HEADS = 8
HID = 2048
TAPS = 31
CAP = 16
EXPERTS = 32
ROWS = EXPERTS * CAP
KEYS = 4096

S_G, S_X, S_R, S_T = 0, 32, 64, 96
S_HM, S_HG = 128, 130
S_Q, S_KV, S_KVP = 132, 140, 148
S_DO, S_DKVP, S_DKVZ, S_DQ = 152, 160, 164, 172
S_DC1, S_DC2, S_DC3 = 180, 188, 192
SEMS = 200

NT = (((1,), (1,)), ((), ()))


def dot(a, b):
    return jnp.dot(a, b, preferred_element_type=F32)


def dot_nt(a, b):
    return lax.dot_general(a, b, NT, preferred_element_type=F32)


def loop(name, first, last, body, init=0):
    with jax.named_scope(name):
        return lax.fori_loop(first, last, body, init)


def rem(a, b):
    return lax.rem(a, jnp.int32(b))


def div(a, b):
    return lax.div(a, jnp.int32(b))


def three_rows(rows, h):
    high = rows[h : h + 1, :].astype(BF16).astype(F32)
    rest = rows[h : h + 1, :] - high
    middle = rest.astype(BF16).astype(F32)
    low = rest - middle
    at = lax.broadcasted_iota(jnp.int32, (16, rows.shape[1]), 0)
    zero = jnp.zeros((16, rows.shape[1]), F32)
    block = jnp.where(at == 0, high, jnp.where(at == 1, middle, jnp.where(at == 2, low, zero)))
    return block.astype(BF16)


def lanes_below(shape, n):
    return lax.broadcasted_iota(jnp.int32, shape, 1) < n


def kernel(
    mid_hbm, up_hbm, q_hbm, k_hbm, v_hbm, attn_hbm, norm_hbm, oproj_hbm, cw_hbm, gates_hbm, ids_hbm,
    slots_hbm, win_hbm, wout_hbm,
    dmid_hbm, dq_hbm, dk_hbm, dv_hbm, dconv_hbm, dgates_hbm,
    mid_ref, up_ref, q_ref, k_ref, v_ref, attn_ref, norm_ref, cw_ref, gates_ref, ids_ref, slots_ref,
    dmid_ref, dq_ref, dk_ref, dv_ref, dconv_ref, dgates_ref,
    win, wout, oproj, wide, gwide, cwf, halo_m, halo_g, gm, pick, sg, sx, rg, rx, upw, hg, rs, rr,
    gs, gr, qs, qr, ks, kva, qz, qn, nrow, kt, pt, dos, dor, doz, don, drow, attn_t, dkv_s, dkv_r,
    dkv0, dkv_z, dkv_o, dqa, dq_s, dq_o, dc_s, dc_r, dc1, dc2, dc3, dcf, tmp, columns,
    dkv2, ssem, rsem, wsem, isem, osem,
):
    grp, ctx = lax.axis_index("grp"), lax.axis_index("ctx")
    ylo, xx = div(grp, 4), rem(grp, 4)
    z, yhi, core = div(ctx, 4), rem(div(ctx, 2), 2), rem(ctx, 2)
    j = rem(ctx, 4)

    def near(dz, dj, in_group=False):
        dz, dj = jnp.int32(dz), jnp.int32(dj)
        dy, dc = div(dj, 2), rem(dj, 2)
        y_other = ylo if in_group else rem(ylo + dy, 2)
        return (
            y_other * 4 + xx,
            rem(z + dz, 8) * 4 + rem(yhi + dy, 2) * 2 + rem(core + dc, 2),
        )

    def along(step):
        return (grp, rem(ctx + step + 32, 32))

    def remote(src, dst, send_at, recv_at, device):
        return pltpu.make_async_remote_copy(
            src_ref=src, dst_ref=dst, send_sem=ssem.at[send_at], recv_sem=rsem.at[recv_at],
            device_id=device, device_id_type=MESH,
        )

    def arrived(ref, recv_at):
        remote(ref, ref, 0, recv_at, along(1)).wait_recv()

    def sent(ref, send_at):
        remote(ref, ref, send_at, 0, along(1)).wait_send()

    def place(k):
        n = div(k, 4)
        odd = rem(n, 2)
        return rem(odd * div(n + 1, 2) + (1 - odd) * (8 - div(n, 2)), 8), rem(k, 4)

    def slot_rows(k):
        return pl.ds(pl.multiple_of(k * CAP, CAP), CAP)

    w_copies = [
        pltpu.make_async_copy(wout_hbm.at[0], wout, wsem.at[0]),
        pltpu.make_async_copy(win_hbm.at[0], win, wsem.at[1]),
        pltpu.make_async_copy(oproj_hbm, oproj, wsem.at[2]),
    ]
    inputs = dict(
        ids=(ids_hbm, ids_ref), slots=(slots_hbm, slots_ref), up=(up_hbm, up_ref), mid=(mid_hbm, mid_ref),
        cw=(cw_hbm, cw_ref), gates=(gates_hbm, gates_ref), norm=(norm_hbm, norm_ref), q=(q_hbm, q_ref),
        attn=(attn_hbm, attn_ref), k=(k_hbm, k_ref), v=(v_hbm, v_ref),
    )
    loads = {name: pltpu.make_async_copy(*pair, isem.at[n]) for n, (name, pair) in enumerate(inputs.items())}
    stores = [
        pltpu.make_async_copy(here, there, osem.at[n])
        for n, (here, there) in enumerate((
            (dmid_ref, dmid_hbm), (dq_ref, dq_hbm), (dk_ref, dk_hbm), (dv_ref, dv_hbm), (dconv_ref, dconv_hbm),
            (dgates_ref, dgates_hbm),
        ))
    ]
    for copy in loads.values():
        copy.start()

    def loaded(*names):
        for name in names:
            loads[name].wait()

    barrier = pltpu.get_barrier_semaphore()

    def greet(k, _):
        dz, dj = place(k)
        pl.semaphore_signal(barrier, inc=1, device_id=near(dz, dj), device_id_type=MESH)
        return 0

    loop("greet", 1, 32, greet)
    for dj in (2, 3):
        pl.semaphore_signal(barrier, inc=1, device_id=near(0, dj, True), device_id_type=MESH)
    for step in (1, -1):
        pl.semaphore_signal(barrier, inc=1, device_id=along(step), device_id_type=MESH)
    for copy in w_copies:
        copy.start()

    loaded("ids", "slots", "up")
    ids, slot = ids_ref[...], slots_ref[...]
    planes_on = (jnp.right_shift(ids, 2) - z + 8) & 7
    in_plane = ((jnp.right_shift(ids, 1) + yhi) & 1) * 2 + ((ids + core) & 1)
    spot = planes_on * 4 + in_plane
    sid = spot * CAP + slot
    at = lax.broadcasted_iota(jnp.int32, (ROWS, FR), 0)
    spread = jnp.where((at == sid[0:1, :]) | (at == sid[1:2, :]), 1.0, 0.0).astype(BF16)

    for n in range(4):
        rows = slice(n * 128, n * 128 + 128)
        sg[rows, :] = dot(spread[rows, :], up_ref[...]).astype(BF16)
    rg[0:CAP, :] = sg[0:CAP, :]

    pl.semaphore_wait(barrier, 35)

    loaded("mid")
    halo_m_out = [
        remote(mid_ref.at[pl.ds(FR - 16, 16)], halo_m.at[0], S_HM, S_HM, along(1)),
        remote(mid_ref.at[pl.ds(0, 16)], halo_m.at[1], S_HM + 1, S_HM + 1, along(-1)),
    ]
    for copy in halo_m_out:
        copy.start()

    def spread_out(src, dst, first):
        def body(k, _):
            dz, dj = place(k)
            here = dz * 4 + dj
            there = rem(8 - dz, 8) * 4 + dj
            remote(
                src.at[slot_rows(here)], dst.at[slot_rows(there)], first + here, first + there, near(dz, dj)
            ).start()
            return 0

        loop("body", 1, 32, body)

    spread_out(sg, rg, S_G)

    loaded("cw", "gates", "norm", "q", "attn", "k", "v")
    cwf[0:TAPS, :] = cw_ref[...].astype(F32)
    norm_t = norm_ref[...]
    tmp[...] = jnp.zeros((FR, 128), F32)
    tmp[0:2, :] = sid.astype(F32)
    tmp[2:4, :] = gates_ref[...]
    columns[...] = jnp.transpose(tmp[...])
    lane = lax.broadcasted_iota(jnp.int32, (FR, ROWS), 1)
    for r in range(2):
        pick[r] = jnp.where(lane == columns[:, r : r + 1].astype(jnp.int32), 1.0, 0.0).astype(BF16)
    for n in range(4):
        cols = slice(n * 128, n * 128 + 128)
        q_t = jnp.transpose(q_ref[:, cols].astype(F32) * 0.125).astype(BF16)
        attn_t[cols, :] = jnp.transpose(attn_ref[:, cols].astype(F32))
        kk, vv = k_ref[:, cols].astype(F32), v_ref[:, cols].astype(F32)
        first = lanes_below((FR, 128), 64)
        ks[2 * n] = jnp.where(first, kk, pltpu.roll(vv, 64, 1)).astype(BF16)
        ks[2 * n + 1] = jnp.where(first, pltpu.roll(kk, 64, 1), vv).astype(BF16)
        for half in range(2):
            h = 2 * n + half
            qs[h * 80 : h * 80 + 64, :] = q_t[half * 64 : half * 64 + 64, :]
            qs[h * 80 + 64 : h * 80 + 80, :] = three_rows(norm_t, h)

    def head_rows(h):
        return pl.ds(pl.multiple_of(h * 80, 16), 80)

    wide[16 : 16 + FR, :] = mid_ref[...].astype(F32)
    for side, copy in enumerate(halo_m_out):
        arrived(halo_m.at[side], S_HM + side)
    not_first = jnp.where(ctx > 0, 1.0, 0.0).astype(F32)
    not_last = jnp.where(ctx < 31, 1.0, 0.0).astype(F32)
    wide[0:16, :] = halo_m[0].astype(F32) * not_first
    wide[16 + FR : 32 + FR, :] = halo_m[1].astype(F32) * not_last

    def lane_tile(i):
        return pl.ds(pl.multiple_of(i * 128, 128), 128)

    def convolve(src, dst, backward):
        def conv_tile(i, _):
            cols = lane_tile(i)
            total = src[pl.ds(16, FR), cols]
            for o in range(1, TAPS + 1):
                tap = TAPS - o if backward else o - 1
                total = total + cwf[pl.ds(tap, 1), cols] * src[pl.ds(o, FR), cols]
            dst[:, cols] = total.astype(BF16)
            return 0

        loop("conv_tile", 0, 8, conv_tile)

    convolve(wide, gm, False)
    for n in range(4):
        rows = slice(n * 128, n * 128 + 128)
        sx[rows, :] = dot(spread[rows, :], gm[...]).astype(BF16)
    rx[0:CAP, :] = sx[0:CAP, :]
    spread_out(sx, rx, S_X)

    w_copies[0].wait()
    w_copies[1].wait()

    def g_arrived(k, _):
        arrived(rg.at[slot_rows(k)], S_G + k)
        return 0

    loop("g_arrived", 1, 32, g_arrived)

    def upward_tile(i, _):
        rows = pl.ds(pl.multiple_of(i * 256, 256), 256)
        upw[:, rows] = dot_nt(rg[...], wout[rows, :])
        return 0

    loop("upward_tile", 0, HID // 256, upward_tile)

    for chunk in (0, 3, 1, 2):
        rows = slice(chunk * 128, chunk * 128 + 128)

        def x_arrived(k, _):
            arrived(rx.at[slot_rows(k)], S_X + k)
            return 0

        loop("x_arrived", max(chunk * 8, 1), chunk * 8 + 8, x_arrived)

        def hidden_tile(i, gate):
            cols = pl.ds(pl.multiple_of(i * 256, 256), 256)
            pre = dot(rx[rows, :], win[:, cols])
            upward = upw[rows, cols]
            sig = jax.nn.sigmoid(pre)
            unit = pre * sig * upward
            hg[:, cols] = (upward * sig * (1.0 + pre * (1.0 - sig))).astype(BF16)
            return gate + unit[:, 0:128] + unit[:, 128:256]

        gate = loop("hidden_tile", 0, HID // 256, hidden_tile, jnp.zeros((FR, 128), F32))
        gate_row = jnp.sum(jnp.transpose(gate), axis=0, keepdims=True).astype(BF16).astype(F32)
        gs[chunk] = gate_row

        def grad_tile(i, _):
            cols = pl.ds(pl.multiple_of(i * 256, 256), 256)
            rs[rows, cols] = dot_nt(hg[...], win[cols, :]).astype(BF16)
            return 0

        loop("grad_tile", 0, D // 256, grad_tile)

        def give_back(k, _):
            dz, dj = div(k, 4), rem(k, 4)
            there = rem(8 - dz, 8) * 4 + dj
            device = near(dz, dj)
            remote(rs.at[slot_rows(k)], rr.at[slot_rows(there)], S_R + k, S_R + there, device).start()
            remote(gs.at[chunk], gr.at[there], S_T + k, S_T + there, device).start()
            return 0

        loop("give_back", max(chunk * 8, 1), chunk * 8 + 8, give_back)
    rr[0:CAP, :] = rs[0:CAP, :]
    gr[0] = gs[0]

    qr[0] = qs[head_rows(z), :]
    kva[0:FR, :] = ks[z]

    def keys_to_planes(dz, _):
        back = 8 - dz
        rows = pl.ds(pl.multiple_of(back * FR, FR), FR)
        remote(ks.at[rem(z + dz, 8)], kva.at[rows], S_KV + dz, S_KV + back, near(dz, 0)).start()
        return 0

    def queries_to_planes(dz, _):
        back = 8 - dz
        remote(qs.at[head_rows(rem(z + dz, 8))], qr.at[back], S_Q + dz, S_Q + back, near(dz, 0)).start()
        return 0

    loop("keys_to_planes", 1, 8, keys_to_planes)
    loop("queries_to_planes", 1, 8, queries_to_planes)

    def r_arrived(k, _):
        arrived(rr.at[slot_rows(k)], S_R + k)
        return 0

    loop("r_arrived", 1, 32, r_arrived)
    for n in range(4):
        cols = slice(n * 256, n * 256 + 256)
        back = rr[:, cols]
        grad = up_ref[:, cols].astype(F32)
        grad = grad + columns[:, 2:3] * dot(pick[0], back)
        grad = grad + columns[:, 3:4] * dot(pick[1], back)
        gm[:, cols] = grad.astype(BF16)

    halo_g_out = [
        remote(gm.at[pl.ds(FR - 16, 16)], halo_g.at[0], S_HG, S_HG, along(1)),
        remote(gm.at[pl.ds(0, 16)], halo_g.at[1], S_HG + 1, S_HG + 1, along(-1)),
    ]
    for copy in halo_g_out:
        copy.start()
    gwide[16 : 16 + FR, :] = gm[...].astype(F32)

    def kv_arrived(k, _):
        arrived(kva.at[pl.ds(pl.multiple_of(k * FR, FR), FR)], S_KV + k)
        return 0

    loop("kv_arrived", 1, 8, kv_arrived)
    own_keys = kva.at[pl.ds(0, 1024)]
    for dj in (2, 1):
        remote(own_keys, kva.at[pl.ds(dj * 1024, 1024)], S_KVP + dj, S_KVP + dj, near(0, dj, True)).start()

    def tap_tile(i, _):
        cols = lane_tile(i)
        here = gwide[pl.ds(16, FR), cols]
        for o in range(1, TAPS + 1):
            part = jnp.sum((wide[pl.ds(o, FR), cols] * here).reshape(16, 8, 128), axis=0)
            dc_s[i, pl.ds(o - 1, 1), :] = jnp.sum(part, axis=0, keepdims=True)
        dc_s[i, pl.ds(TAPS, 1), :] = jnp.zeros((1, 128), F32)
        return 0

    loop("tap_tile", 0, 8, tap_tile)

    def taps_out(dz, _):
        remote(dc_s.at[rem(z + dz, 8)], dc_r.at[8 - dz], S_DC1 + dz, S_DC1 + 8 - dz, near(dz, 0)).start()
        return 0

    for side in range(2):
        arrived(halo_g.at[side], S_HG + side)
    gwide[0:16, :] = halo_g[0].astype(F32) * not_first
    gwide[16 + FR : 32 + FR, :] = halo_g[1].astype(F32) * not_last
    convolve(gwide, dmid_ref, True)
    stores[0].start()

    w_copies[2].wait()
    grad_out = dot_nt(oproj[...], dmid_ref[...]).astype(BF16)
    delta = jnp.sum((grad_out.astype(F32) * attn_t[...]).reshape(HEADS, 64, FR), axis=1)
    for h in range(HEADS):
        dos[h * 80 : h * 80 + 64, :] = grad_out[h * 64 : h * 64 + 64, :]
        dos[h * 80 + 64 : h * 80 + 80, :] = three_rows(delta, h)
    dor[0] = dos[head_rows(z), :]

    def dout_to_planes(dz, _):
        back = 8 - dz
        remote(dos.at[head_rows(rem(z + dz, 8))], dor.at[back], S_DO + dz, S_DO + back, near(dz, 0)).start()
        return 0

    loop("dout_to_planes", 1, 8, dout_to_planes)
    loop("taps_out", 1, 8, taps_out)

    def q_arrived(k, _):
        arrived(qr.at[k], S_Q + k)
        return 0

    loop("q_arrived", 1, 8, q_arrived)
    qz[64:128, :] = jnp.zeros((64, 1024), BF16)
    for b in range(8):
        cols = slice(b * 128, b * 128 + 128)
        qz[0:64, cols] = qr[b, 0:64, :]
        nrow[:, cols] = jnp.sum(qr[b, 64:80, :].astype(F32), axis=0, keepdims=True)
        qn[cols, :] = jnp.transpose(qz[:, cols].astype(F32)).astype(BF16)
    for dj in range(4):
        if dj:
            arrived(kva.at[pl.ds(dj * 1024, 1024)], S_KVP + dj)
        if dj == 2:
            remote(
                kva.at[pl.ds(2048, 1024)], kva.at[pl.ds(3072, 1024)], S_KVP + 3, S_KVP + 3, near(0, 1)
            ).start()

        def prob_tile(i, _):
            rows = pl.ds(pl.multiple_of(i * 256, 256), 256)
            tile = kva[rows, :]
            kt[:, rows] = jnp.transpose(tile.astype(F32))[0:64, :].astype(BF16)
            pt[rows, :] = jnp.exp(dot(tile, qz[...]) - nrow[...]).astype(BF16)
            return 0

        loop("prob_tile", dj * 4, dj * 4 + 4, prob_tile)

    def do_arrived(k, _):
        arrived(dor.at[k], S_DO + k)
        return 0

    loop("do_arrived", 1, 8, do_arrived)
    doz[0:64, :] = jnp.zeros((64, 1024), BF16)
    for b in range(8):
        cols = slice(b * 128, b * 128 + 128)
        doz[64:128, cols] = dor[b, 0:64, :]
        drow[:, cols] = jnp.sum(dor[b, 64:80, :].astype(F32), axis=0, keepdims=True)
        don[cols, :] = jnp.transpose(doz[:, cols].astype(F32)).astype(BF16)
    dqa[...] = jnp.zeros((64, 1024), F32)

    for dj in (3, 2, 1, 0):

        def score_tile(i, _):
            at = pl.multiple_of(i * 256, 256)
            rows = pl.ds(pl.multiple_of(dj * 1024 + at, 256), 256)
            prob = pt[rows, :]
            dprob = dot(kva[rows, :], doz[...]) - drow[...]
            score = (prob.astype(F32) * dprob).astype(BF16)
            both_grads = dot(score, qn[...]) + dot(prob, don[...])
            if dj % 2:
                dkv_s[dj - 1, pl.ds(at, 256), :] = both_grads.astype(BF16)
            else:
                (dkv2 if dj else dkv0)[pl.ds(at, 256), :] = both_grads
            dqa[...] += dot(kt[:, rows], score)
            return 0

        loop("score_tile", 0, 4, score_tile)
        if dj == 2:
            arrived(dkv_r.at[2], S_DKVP + 3)

            def join_tile(i, _):
                rows = pl.ds(pl.multiple_of(i * 256, 256), 256)
                dkv_s[1, rows, :] = (dkv2[rows, :] + dkv_r[2, rows, :].astype(F32)).astype(BF16)
                return 0

            loop("join_tile", 0, 4, join_tile)
        if dj:
            device = near(0, 2, True) if dj == 2 else near(0, 1)
            remote(dkv_s.at[dj - 1], dkv_r.at[dj - 1], S_DKVP + dj, S_DKVP + dj, device).start()

    for b in range(8):
        dq_s[b] = (dqa[:, b * 128 : b * 128 + 128] * 0.125).astype(BF16)
    z_rows = pl.ds(pl.multiple_of(z * 64, 64), 64)
    dq_o[z_rows, :] = dq_s[0]

    def dq_home(dz, _):
        remote(dq_s.at[dz], dq_o.at[z_rows], S_DQ + dz, S_DQ + 8 - dz, near(dz, 0)).start()
        return 0

    loop("dq_home", 1, 8, dq_home)

    def dc1_arrived(k, _):
        arrived(dc_r.at[k], S_DC1 + k)
        return 0

    loop("dc1_arrived", 1, 8, dc1_arrived)
    taps = dc_s[z]
    for b in range(1, 8):
        taps = taps + dc_r[b]
    dc1[...] = taps
    dc2[j] = taps
    for dj in (2, 3, 1):
        remote(dc1, dc2.at[j], S_DC2 + dj, S_DC2 + dj, near(0, dj, True)).start()

    for dj in (1, 2):
        arrived(dkv_r.at[dj - 1], S_DKVP + dj)

    def sum_keys(k, _):
        n = rem(k + 1, 8)
        rows = pl.ds(pl.multiple_of(n * FR, FR), FR)
        total = dkv0[rows, :]
        for p in range(2):
            total = total + dkv_r[p, rows, :].astype(F32)
        dkv_z[n] = total.astype(BF16)

        @pl.when(n > 0)
        def _():
            remote(dkv_z.at[n], dkv_o.at[z], S_DKVZ + n, S_DKVZ + rem(8 - n, 8), near(n, 0)).start()

        return 0

    loop("sum_keys", 0, 8, sum_keys)
    dkv_o[z] = dkv_z[0]

    for dj in (1, 2, 3):
        arrived(dc1, S_DC2 + dj)
    dc3[...] = (dc2[0] + dc2[1]) + (dc2[2] + dc2[3])
    dcf[z] = dc3[...]

    def taps_home(dz, _):
        remote(dc3, dcf.at[z], S_DC3 + dz, S_DC3 + 8 - dz, near(dz, 0)).start()
        return 0

    loop("taps_home", 1, 8, taps_home)

    def t_arrived(k, _):
        arrived(gr.at[k], S_T + k)
        return 0

    loop("t_arrived", 1, 32, t_arrived)
    tmp[...] = jnp.zeros((FR, 128), F32)
    for k in range(EXPERTS):
        tmp[k : k + 1, :] = gr[k]
    units = jnp.transpose(tmp[...]).astype(BF16)
    at = lax.broadcasted_iota(jnp.int32, (128, FR), 0)
    for r in range(2):
        line = dot(units, jnp.where(at == spot[r : r + 1, :], 1.0, 0.0).astype(BF16))
        own = at == (sid[r : r + 1, :] & 127)
        dgates_ref[r : r + 1, :] = jnp.sum(jnp.where(own, line, 0.0), axis=0, keepdims=True).astype(BF16)
    stores[5].start()

    def dq_arrived(k, _):
        arrived(dq_s.at[k], S_DQ + k)
        return 0

    loop("dq_arrived", 1, 8, dq_arrived)
    for n in range(4):
        cols = slice(n * 128, n * 128 + 128)
        dq_ref[:, cols] = jnp.transpose(dq_o[cols, :].astype(F32)).astype(BF16)
    stores[1].start()

    def dkv_arrived(k, _):
        arrived(dkv_z.at[k], S_DKVZ + k)
        return 0

    loop("dkv_arrived", 1, 8, dkv_arrived)
    for n in range(4):
        cols = slice(n * 128, n * 128 + 128)
        first = lanes_below((FR, 128), 64)
        one, two = dkv_o[2 * n].astype(F32), dkv_o[2 * n + 1].astype(F32)
        dk_ref[:, cols] = jnp.where(first, one, pltpu.roll(two, 64, 1)).astype(BF16)
        dv_ref[:, cols] = jnp.where(first, pltpu.roll(one, 64, 1), two).astype(BF16)
    stores[2].start()
    stores[3].start()

    def dc3_arrived(k, _):
        arrived(dc3, S_DC3 + k)
        return 0

    loop("dc3_arrived", 1, 8, dc3_arrived)
    for n in range(8):
        dconv_ref[:, n * 128 : n * 128 + 128] = dcf[n, 0:TAPS, :]
    stores[4].start()

    def rows_left(k, _):
        for first in (S_G, S_X, S_R):
            sent(sg.at[slot_rows(k)], first + k)
        sent(gr.at[k], S_T + k)
        return 0

    loop("rows_left", 1, 32, rows_left)

    def blocks_left(k, _):
        sent(qr.at[k], S_Q + k)
        sent(ks.at[k], S_KV + k)
        sent(dor.at[k], S_DO + k)
        sent(dkv_z.at[k], S_DKVZ + k)
        sent(dq_s.at[k], S_DQ + k)
        sent(dc_r.at[k], S_DC1 + k)
        sent(dc3, S_DC3 + k)
        return 0

    loop("blocks_left", 1, 8, blocks_left)
    for copy in halo_m_out + halo_g_out:
        copy.wait_send()
    for dj in (1, 2, 3):
        sent(kva.at[pl.ds(0, 1024)], S_KVP + dj)
        sent(dkv_s.at[dj - 1], S_DKVP + dj)
        sent(dc1, S_DC2 + dj)
    for copy in stores:
        copy.wait()


def store(*refs):
    held, sems = refs[12:18], refs[18]
    ins = [pltpu.make_async_copy(refs[n], held[n], sems.at[n]) for n in range(6)]
    outs = [pltpu.make_async_copy(held[n], refs[6 + n], sems.at[6 + n]) for n in range(6)]
    for copy in ins:
        copy.start()
    for first, second in zip(ins, outs):
        first.wait()
        second.start()
    for copy in outs:
        copy.wait()


def on_device(*args):
    args = list(args)
    for n in (6, 9, 10, 11):
        args[n] = args[n].T
    anywhere = pl.BlockSpec(memory_space=pl.ANY)
    V = pltpu.VMEM
    scratch = [
        V((FR, D), BF16), V((FR, D), BF16), V((FR, 512), BF16), V((FR, 512), BF16), V((FR, 512), BF16), V((FR, 512), BF16),
        V((HEADS, FR), F32), V((TAPS, D), BF16), V((2, FR), F32), V((2, FR), jnp.int32), V((2, FR), jnp.int32),
        V((FR, D), BF16), V((FR, 512), BF16), V((FR, 512), BF16), V((FR, 512), BF16), V((TAPS, D), F32), V((2, FR), BF16),
        V((D, HID), BF16), V((HID, D), BF16), V((512, D), BF16),
        V((160, D), F32), V((160, D), F32), V((32, D), F32),
        V((2, 16, D), BF16), V((2, 16, D), BF16), V((FR, D), BF16), V((2, FR, ROWS), BF16),
        V((ROWS, D), BF16), V((ROWS, D), BF16), V((ROWS, D), BF16), V((ROWS, D), BF16),
        V((ROWS, HID), F32), V((FR, HID), BF16), V((ROWS, D), BF16), V((ROWS, D), BF16),
        V((4, 1, 128), F32), V((EXPERTS, 1, 128), F32),
        V((640, 128), BF16), V((8, 80, 128), BF16), V((8, FR, 128), BF16), V((KEYS, 128), BF16),
        V((128, 1024), BF16), V((1024, 128), BF16), V((1, 1024), F32), V((64, KEYS), BF16), V((KEYS, 1024), BF16),
        V((640, 128), BF16), V((8, 80, 128), BF16), V((128, 1024), BF16), V((1024, 128), BF16), V((1, 1024), F32),
        V((512, FR), F32), V((3, 1024, 128), BF16), V((3, 1024, 128), BF16),
        V((1024, 128), F32), V((8, FR, 128), BF16), V((8, FR, 128), BF16),
        V((64, 1024), F32), V((8, 64, 128), BF16), V((512, 128), BF16),
        V((8, 32, 128), F32), V((8, 32, 128), F32), V((32, 128), F32), V((4, 32, 128), F32), V((32, 128), F32),
        V((8, 32, 128), F32), V((FR, 128), F32), V((FR, 128), F32),
        V((1024, 128), F32),
        pltpu.SemaphoreType.DMA((SEMS,)), pltpu.SemaphoreType.DMA((SEMS,)), pltpu.SemaphoreType.DMA((3,)),
        pltpu.SemaphoreType.DMA((11,)), pltpu.SemaphoreType.DMA((6,)),
    ]
    shape = jax.ShapeDtypeStruct
    out_shape = (
        shape((FR, D), BF16), shape((FR, 512), BF16), shape((FR, 512), BF16), shape((FR, 512), BF16),
        shape((TAPS, D), F32), shape((2, FR), BF16),
    )
    found = pl.pallas_call(
        kernel,
        out_shape=out_shape,
        in_specs=[anywhere] * 14,
        out_specs=(anywhere,) * 6,
        scratch_shapes=scratch,
        compiler_params=pltpu.CompilerParams(
            collective_id=0, has_side_effects=True, vmem_limit_bytes=58 * 1024 * 1024
        ),
        name="conformer_backward",
    )(*args)
    results = pl.pallas_call(
        store,
        out_shape=out_shape,
        in_specs=[anywhere] * 6,
        out_specs=(anywhere,) * 6,
        scratch_shapes=[V(o.shape, o.dtype) for o in out_shape] + [pltpu.SemaphoreType.DMA((12,))],
        compiler_params=pltpu.CompilerParams(vmem_limit_bytes=60 * 1024 * 1024),
        name="store",
    )(*found)
    return (*results[:5], results[5].T)


def solution(mesh):
    frames = P(("grp", "ctx"), None)
    in_specs = (frames,) * 7 + (P(), P()) + (frames,) * 3 + (P("ctx", None, None),) * 2
    out_specs = (frames,) * 4 + (P("grp", None), frames)
    return jax.shard_map(on_device, mesh=mesh, in_specs=in_specs, out_specs=out_specs, check_vma=False)
```

```python
import jax
import jax.numpy as jnp
from jax import lax
from jax.experimental import pallas as pl
from jax.experimental.pallas import tpu as pltpu
from jax.sharding import PartitionSpec as P

MESH = pl.DeviceIdType.MESH
F32 = jnp.float32
BF16 = jnp.bfloat16

FR = 128
D = 1024
HEADS = 8
HID = 2048
TAPS = 31
CAP = 16
EXPERTS = 32
ROWS = EXPERTS * CAP
KEYS = 4096

S_G, S_X, S_R, S_T = 0, 32, 64, 96
S_HM, S_HG = 128, 130
S_Q, S_KV, S_KVP = 132, 140, 148
S_DO, S_DKVP, S_DKVZ, S_DQ = 152, 160, 164, 172
S_DC1, S_DC2, S_DC3 = 180, 188, 192
S_DKVP2 = 200
SEMS = 204

NT = (((1,), (1,)), ((), ()))


def dot(a, b):
    return jnp.dot(a, b, preferred_element_type=F32)


def dot_nt(a, b):
    return lax.dot_general(a, b, NT, preferred_element_type=F32)


def loop(name, first, last, body, init=0):
    with jax.named_scope(name):
        return lax.fori_loop(first, last, body, init)


def rem(a, b):
    return lax.rem(a, jnp.int32(b))


def div(a, b):
    return lax.div(a, jnp.int32(b))


def three_rows(rows, h):
    high = rows[h : h + 1, :].astype(BF16).astype(F32)
    rest = rows[h : h + 1, :] - high
    middle = rest.astype(BF16).astype(F32)
    low = rest - middle
    at = lax.broadcasted_iota(jnp.int32, (16, rows.shape[1]), 0)
    zero = jnp.zeros((16, rows.shape[1]), F32)
    block = jnp.where(at == 0, high, jnp.where(at == 1, middle, jnp.where(at == 2, low, zero)))
    return block.astype(BF16)


def lanes_below(shape, n):
    return lax.broadcasted_iota(jnp.int32, shape, 1) < n


def kernel(
    mid_hbm, up_hbm, q_hbm, k_hbm, v_hbm, attn_hbm, norm_hbm, oproj_hbm, cw_hbm, gates_hbm, ids_hbm,
    slots_hbm, win_hbm, wout_hbm,
    dmid_hbm, dq_hbm, dk_hbm, dv_hbm, dconv_hbm, dgates_hbm,
    mid_ref, up_ref, q_ref, k_ref, v_ref, attn_ref, norm_ref, cw_ref, gates_ref, ids_ref, slots_ref,
    dmid_ref, dq_ref, dk_ref, dv_ref, dconv_ref, dgates_ref,
    win, wout, oproj, wide, gwide, cwf, halo_m, halo_g, gm, pick, sg, sx, rg, rx, upw, hg, rs, rr,
    gs, gr, qs, qr, ks, kva, qz, qn, nrow, kt, pt, dos, dor, doz, don, drow, attn_t, dkv_s, dkv_r,
    dkv0, dkv_z, dkv_o, dqa, dq_s, dq_o, dc_s, dc_r, dc1, dc2, dc3, dcf, tmp, columns,
    dkv2, ssem, rsem, wsem, isem, osem,
):
    grp, ctx = lax.axis_index("grp"), lax.axis_index("ctx")
    ylo, xx = div(grp, 4), rem(grp, 4)
    z, yhi, core = div(ctx, 4), rem(div(ctx, 2), 2), rem(ctx, 2)
    j = rem(ctx, 4)

    def near(dz, dj, in_group=False):
        dz, dj = jnp.int32(dz), jnp.int32(dj)
        dy, dc = div(dj, 2), rem(dj, 2)
        y_other = ylo if in_group else rem(ylo + dy, 2)
        return (
            y_other * 4 + xx,
            rem(z + dz, 8) * 4 + rem(yhi + dy, 2) * 2 + rem(core + dc, 2),
        )

    def along(step):
        return (grp, rem(ctx + step + 32, 32))

    def remote(src, dst, send_at, recv_at, device):
        return pltpu.make_async_remote_copy(
            src_ref=src, dst_ref=dst, send_sem=ssem.at[send_at], recv_sem=rsem.at[recv_at],
            device_id=device, device_id_type=MESH,
        )

    def arrived(ref, recv_at):
        remote(ref, ref, 0, recv_at, along(1)).wait_recv()

    def sent(ref, send_at):
        remote(ref, ref, send_at, 0, along(1)).wait_send()

    def place(k):
        n = div(k, 4)
        odd = rem(n, 2)
        return rem(odd * div(n + 1, 2) + (1 - odd) * (8 - div(n, 2)), 8), rem(k, 4)

    def slot_rows(k):
        return pl.ds(pl.multiple_of(k * CAP, CAP), CAP)

    w_copies = [
        pltpu.make_async_copy(wout_hbm.at[0], wout, wsem.at[0]),
        pltpu.make_async_copy(win_hbm.at[0], win, wsem.at[1]),
        pltpu.make_async_copy(oproj_hbm, oproj, wsem.at[2]),
    ]
    inputs = dict(
        ids=(ids_hbm, ids_ref), slots=(slots_hbm, slots_ref), up=(up_hbm, up_ref), mid=(mid_hbm, mid_ref),
        cw=(cw_hbm, cw_ref), gates=(gates_hbm, gates_ref), norm=(norm_hbm, norm_ref), q=(q_hbm, q_ref),
        attn=(attn_hbm, attn_ref), k=(k_hbm, k_ref), v=(v_hbm, v_ref),
    )
    loads = {name: pltpu.make_async_copy(*pair, isem.at[n]) for n, (name, pair) in enumerate(inputs.items())}
    stores = [
        pltpu.make_async_copy(here, there, osem.at[n])
        for n, (here, there) in enumerate((
            (dmid_ref, dmid_hbm), (dq_ref, dq_hbm), (dk_ref, dk_hbm), (dv_ref, dv_hbm), (dconv_ref, dconv_hbm),
            (dgates_ref, dgates_hbm),
        ))
    ]
    for copy in loads.values():
        copy.start()

    def loaded(*names):
        for name in names:
            loads[name].wait()

    barrier = pltpu.get_barrier_semaphore()

    def greet(k, _):
        dz, dj = place(k)
        pl.semaphore_signal(barrier, inc=1, device_id=near(dz, dj), device_id_type=MESH)
        return 0

    loop("greet", 1, 32, greet)
    for dj in (2, 3):
        pl.semaphore_signal(barrier, inc=1, device_id=near(0, dj, True), device_id_type=MESH)
    for step in (1, -1):
        pl.semaphore_signal(barrier, inc=1, device_id=along(step), device_id_type=MESH)
    for copy in w_copies:
        copy.start()

    loaded("ids", "slots", "up")
    ids, slot = ids_ref[...], slots_ref[...]
    planes_on = (jnp.right_shift(ids, 2) - z + 8) & 7
    in_plane = ((jnp.right_shift(ids, 1) + yhi) & 1) * 2 + ((ids + core) & 1)
    spot = planes_on * 4 + in_plane
    sid = spot * CAP + slot
    at = lax.broadcasted_iota(jnp.int32, (ROWS, FR), 0)
    spread = jnp.where((at == sid[0:1, :]) | (at == sid[1:2, :]), 1.0, 0.0).astype(BF16)

    for n in range(4):
        rows = slice(n * 128, n * 128 + 128)
        sg[rows, :] = dot(spread[rows, :], up_ref[...]).astype(BF16)
    rg[0:CAP, :] = sg[0:CAP, :]

    pl.semaphore_wait(barrier, 35)

    loaded("mid")
    halo_m_out = [
        remote(mid_ref.at[pl.ds(FR - 16, 16)], halo_m.at[0], S_HM, S_HM, along(1)),
        remote(mid_ref.at[pl.ds(0, 16)], halo_m.at[1], S_HM + 1, S_HM + 1, along(-1)),
    ]
    for copy in halo_m_out:
        copy.start()

    def spread_out(src, dst, first):
        def body(k, _):
            dz, dj = place(k)
            here = dz * 4 + dj
            there = rem(8 - dz, 8) * 4 + dj
            remote(
                src.at[slot_rows(here)], dst.at[slot_rows(there)], first + here, first + there, near(dz, dj)
            ).start()
            return 0

        loop("body", 1, 32, body)

    spread_out(sg, rg, S_G)

    loaded("cw", "gates", "norm", "q", "attn", "k", "v")
    cwf[0:TAPS, :] = cw_ref[...].astype(F32)
    norm_t = norm_ref[...]
    tmp[...] = jnp.zeros((FR, 128), F32)
    tmp[0:2, :] = sid.astype(F32)
    tmp[2:4, :] = gates_ref[...]
    columns[...] = jnp.transpose(tmp[...])
    lane = lax.broadcasted_iota(jnp.int32, (FR, ROWS), 1)
    for r in range(2):
        pick[r] = jnp.where(lane == columns[:, r : r + 1].astype(jnp.int32), 1.0, 0.0).astype(BF16)
    for n in range(4):
        cols = slice(n * 128, n * 128 + 128)
        q_t = jnp.transpose(q_ref[:, cols].astype(F32) * 0.125).astype(BF16)
        attn_t[cols, :] = jnp.transpose(attn_ref[:, cols].astype(F32))
        kk, vv = k_ref[:, cols].astype(F32), v_ref[:, cols].astype(F32)
        first = lanes_below((FR, 128), 64)
        ks[2 * n] = jnp.where(first, kk, pltpu.roll(vv, 64, 1)).astype(BF16)
        ks[2 * n + 1] = jnp.where(first, pltpu.roll(kk, 64, 1), vv).astype(BF16)
        for half in range(2):
            h = 2 * n + half
            qs[h * 80 : h * 80 + 64, :] = q_t[half * 64 : half * 64 + 64, :]
            qs[h * 80 + 64 : h * 80 + 80, :] = three_rows(norm_t, h)

    def head_rows(h):
        return pl.ds(pl.multiple_of(h * 80, 16), 80)

    wide[16 : 16 + FR, :] = mid_ref[...].astype(F32)
    for side, copy in enumerate(halo_m_out):
        arrived(halo_m.at[side], S_HM + side)
    not_first = jnp.where(ctx > 0, 1.0, 0.0).astype(F32)
    not_last = jnp.where(ctx < 31, 1.0, 0.0).astype(F32)
    wide[0:16, :] = halo_m[0].astype(F32) * not_first
    wide[16 + FR : 32 + FR, :] = halo_m[1].astype(F32) * not_last

    def lane_tile(i):
        return pl.ds(pl.multiple_of(i * 128, 128), 128)

    def convolve(src, dst, backward):
        def conv_tile(i, _):
            cols = lane_tile(i)
            total = src[pl.ds(16, FR), cols]
            for o in range(1, TAPS + 1):
                tap = TAPS - o if backward else o - 1
                total = total + cwf[pl.ds(tap, 1), cols] * src[pl.ds(o, FR), cols]
            dst[:, cols] = total.astype(BF16)
            return 0

        loop("conv_tile", 0, 8, conv_tile)

    convolve(wide, gm, False)
    for n in range(4):
        rows = slice(n * 128, n * 128 + 128)
        sx[rows, :] = dot(spread[rows, :], gm[...]).astype(BF16)
    rx[0:CAP, :] = sx[0:CAP, :]
    spread_out(sx, rx, S_X)

    w_copies[0].wait()
    w_copies[1].wait()

    def g_arrived(k, _):
        arrived(rg.at[slot_rows(k)], S_G + k)
        return 0

    loop("g_arrived", 1, 32, g_arrived)

    def upward_tile(i, _):
        rows = pl.ds(pl.multiple_of(i * 256, 256), 256)
        upw[:, rows] = dot_nt(rg[...], wout[rows, :])
        return 0

    loop("upward_tile", 0, HID // 256, upward_tile)

    for chunk in (0, 3, 1, 2):
        rows = slice(chunk * 128, chunk * 128 + 128)

        def x_arrived(k, _):
            arrived(rx.at[slot_rows(k)], S_X + k)
            return 0

        loop("x_arrived", max(chunk * 8, 1), chunk * 8 + 8, x_arrived)

        def hidden_tile(i, gate):
            cols = pl.ds(pl.multiple_of(i * 256, 256), 256)
            pre = dot(rx[rows, :], win[:, cols])
            upward = upw[rows, cols]
            sig = jax.nn.sigmoid(pre)
            unit = pre * sig * upward
            hg[:, cols] = (upward * sig * (1.0 + pre * (1.0 - sig))).astype(BF16)
            return gate + unit[:, 0:128] + unit[:, 128:256]

        gate = loop("hidden_tile", 0, HID // 256, hidden_tile, jnp.zeros((FR, 128), F32))
        gate_row = jnp.sum(jnp.transpose(gate), axis=0, keepdims=True).astype(BF16).astype(F32)
        gs[chunk] = gate_row

        def grad_tile(i, _):
            cols = pl.ds(pl.multiple_of(i * 256, 256), 256)
            rs[rows, cols] = dot_nt(hg[...], win[cols, :]).astype(BF16)
            return 0

        loop("grad_tile", 0, D // 256, grad_tile)

        def give_back(k, _):
            dz, dj = div(k, 4), rem(k, 4)
            there = rem(8 - dz, 8) * 4 + dj
            device = near(dz, dj)
            remote(rs.at[slot_rows(k)], rr.at[slot_rows(there)], S_R + k, S_R + there, device).start()
            remote(gs.at[chunk], gr.at[there], S_T + k, S_T + there, device).start()
            return 0

        loop("give_back", max(chunk * 8, 1), chunk * 8 + 8, give_back)
    rr[0:CAP, :] = rs[0:CAP, :]
    gr[0] = gs[0]

    qr[0] = qs[head_rows(z), :]
    kva[0:FR, :] = ks[z]

    def keys_to_planes(dz, _):
        back = 8 - dz
        rows = pl.ds(pl.multiple_of(back * FR, FR), FR)
        remote(ks.at[rem(z + dz, 8)], kva.at[rows], S_KV + dz, S_KV + back, near(dz, 0)).start()
        return 0

    def queries_to_planes(dz, _):
        back = 8 - dz
        remote(qs.at[head_rows(rem(z + dz, 8))], qr.at[back], S_Q + dz, S_Q + back, near(dz, 0)).start()
        return 0

    loop("keys_to_planes", 1, 8, keys_to_planes)
    loop("queries_to_planes", 1, 8, queries_to_planes)

    def r_arrived(k, _):
        arrived(rr.at[slot_rows(k)], S_R + k)
        return 0

    loop("r_arrived", 1, 32, r_arrived)
    for n in range(4):
        cols = slice(n * 256, n * 256 + 256)
        back = rr[:, cols]
        grad = up_ref[:, cols].astype(F32)
        grad = grad + columns[:, 2:3] * dot(pick[0], back)
        grad = grad + columns[:, 3:4] * dot(pick[1], back)
        gm[:, cols] = grad.astype(BF16)

    halo_g_out = [
        remote(gm.at[pl.ds(FR - 16, 16)], halo_g.at[0], S_HG, S_HG, along(1)),
        remote(gm.at[pl.ds(0, 16)], halo_g.at[1], S_HG + 1, S_HG + 1, along(-1)),
    ]
    for copy in halo_g_out:
        copy.start()
    gwide[16 : 16 + FR, :] = gm[...].astype(F32)

    def kv_arrived(k, _):
        arrived(kva.at[pl.ds(pl.multiple_of(k * FR, FR), FR)], S_KV + k)
        return 0

    loop("kv_arrived", 1, 8, kv_arrived)
    own_keys = kva.at[pl.ds(0, 1024)]
    for dj in (2, 1):
        remote(own_keys, kva.at[pl.ds(dj * 1024, 1024)], S_KVP + dj, S_KVP + dj, near(0, dj, True)).start()

    def tap_tile(i, _):
        cols = lane_tile(i)
        here = gwide[pl.ds(16, FR), cols]
        for o in range(1, TAPS + 1):
            part = jnp.sum((wide[pl.ds(o, FR), cols] * here).reshape(16, 8, 128), axis=0)
            dc_s[i, pl.ds(o - 1, 1), :] = jnp.sum(part, axis=0, keepdims=True)
        dc_s[i, pl.ds(TAPS, 1), :] = jnp.zeros((1, 128), F32)
        return 0

    loop("tap_tile", 0, 8, tap_tile)

    def taps_out(dz, _):
        remote(dc_s.at[rem(z + dz, 8)], dc_r.at[8 - dz], S_DC1 + dz, S_DC1 + 8 - dz, near(dz, 0)).start()
        return 0

    for side in range(2):
        arrived(halo_g.at[side], S_HG + side)
    gwide[0:16, :] = halo_g[0].astype(F32) * not_first
    gwide[16 + FR : 32 + FR, :] = halo_g[1].astype(F32) * not_last
    convolve(gwide, dmid_ref, True)
    stores[0].start()

    w_copies[2].wait()
    grad_out = dot_nt(oproj[...], dmid_ref[...]).astype(BF16)
    delta = jnp.sum((grad_out.astype(F32) * attn_t[...]).reshape(HEADS, 64, FR), axis=1)
    for h in range(HEADS):
        dos[h * 80 : h * 80 + 64, :] = grad_out[h * 64 : h * 64 + 64, :]
        dos[h * 80 + 64 : h * 80 + 80, :] = three_rows(delta, h)
    dor[0] = dos[head_rows(z), :]

    def dout_to_planes(dz, _):
        back = 8 - dz
        remote(dos.at[head_rows(rem(z + dz, 8))], dor.at[back], S_DO + dz, S_DO + back, near(dz, 0)).start()
        return 0

    loop("dout_to_planes", 1, 8, dout_to_planes)
    loop("taps_out", 1, 8, taps_out)

    def q_arrived(k, _):
        arrived(qr.at[k], S_Q + k)
        return 0

    loop("q_arrived", 1, 8, q_arrived)
    qz[64:128, :] = jnp.zeros((64, 1024), BF16)
    for b in range(8):
        cols = slice(b * 128, b * 128 + 128)
        qz[0:64, cols] = qr[b, 0:64, :]
        nrow[:, cols] = jnp.sum(qr[b, 64:80, :].astype(F32), axis=0, keepdims=True)
        qn[cols, :] = jnp.transpose(qz[:, cols].astype(F32)).astype(BF16)
    for dj in range(4):
        if dj:
            arrived(kva.at[pl.ds(dj * 1024, 1024)], S_KVP + dj)
        if dj == 2:
            remote(
                kva.at[pl.ds(2048, 1024)], kva.at[pl.ds(3072, 1024)], S_KVP + 3, S_KVP + 3, near(0, 1)
            ).start()

        def prob_tile(i, _):
            rows = pl.ds(pl.multiple_of(i * 256, 256), 256)
            tile = kva[rows, :]
            kt[:, rows] = jnp.transpose(tile.astype(F32))[0:64, :].astype(BF16)
            pt[rows, :] = jnp.exp(dot(tile, qz[...]) - nrow[...]).astype(BF16)
            return 0

        loop("prob_tile", dj * 4, dj * 4 + 4, prob_tile)

    def dc1_arrived(k, _):
        arrived(dc_r.at[k], S_DC1 + k)
        return 0

    loop("dc1_arrived", 1, 8, dc1_arrived)
    taps = dc_s[z]
    for b in range(1, 8):
        taps = taps + dc_r[b]
    dc1[...] = taps
    dc2[j] = taps
    for dj in (2, 3, 1):
        remote(dc1, dc2.at[j], S_DC2 + dj, S_DC2 + dj, near(0, dj, True)).start()

    def do_arrived(k, _):
        arrived(dor.at[k], S_DO + k)
        return 0

    loop("do_arrived", 1, 8, do_arrived)
    doz[0:64, :] = jnp.zeros((64, 1024), BF16)
    for b in range(8):
        cols = slice(b * 128, b * 128 + 128)
        doz[64:128, cols] = dor[b, 0:64, :]
        drow[:, cols] = jnp.sum(dor[b, 64:80, :].astype(F32), axis=0, keepdims=True)
        don[cols, :] = jnp.transpose(doz[:, cols].astype(F32)).astype(BF16)
    dqa[...] = jnp.zeros((64, 1024), F32)

    def sum_blocks(half):
        first = S_DKVP2 if half else S_DKVP
        part = pl.ds(half * 512, 512)
        for dj in (1, 2):
            arrived(dkv_r.at[dj - 1, part], first + dj)
        for m, n in enumerate(((2, 3, 4, 5), (0, 1, 6, 7))[half]):
            rows = slice(half * 512 + m * FR, half * 512 + m * FR + FR)
            total = dkv0[rows, :] + dkv_r[0, rows, :].astype(F32) + dkv_r[1, rows, :].astype(F32)
            dkv_z[n] = total.astype(BF16)
            if n:
                remote(dkv_z.at[n], dkv_o.at[z], S_DKVZ + n, S_DKVZ + 8 - n, near(n, 0)).start()

    for half in range(2):
        first = S_DKVP2 if half else S_DKVP
        part = pl.ds(half * 512, 512)
        for dj in (3, 2, 1, 0):

            def score_tile(i, _):
                tile_at = i * 3 if half else i + 1
                rows = pl.ds(pl.multiple_of(dj * 1024 + tile_at * 256, 256), 256)
                kept = pl.ds(pl.multiple_of(half * 512 + i * 256, 256), 256)
                prob = pt[rows, :]
                dprob = dot(kva[rows, :], doz[...]) - drow[...]
                score = (prob.astype(F32) * dprob).astype(BF16)
                both_grads = dot(score, qn[...]) + dot(prob, don[...])
                if dj % 2:
                    dkv_s[dj - 1, kept, :] = both_grads.astype(BF16)
                else:
                    (dkv2 if dj else dkv0)[kept, :] = both_grads
                dqa[...] += dot(kt[:, rows], score)
                return 0

            loop("score_tile", 0, 2, score_tile)
            if dj == 2:
                arrived(dkv_r.at[2, part], first + 3)

                def join_tile(i, _):
                    rows = pl.ds(pl.multiple_of(half * 512 + i * 256, 256), 256)
                    dkv_s[1, rows, :] = (dkv2[rows, :] + dkv_r[2, rows, :].astype(F32)).astype(BF16)
                    return 0

                loop("join_tile", 0, 2, join_tile)
            if dj:
                device = near(0, 2, True) if dj == 2 else near(0, 1)
                remote(
                    dkv_s.at[dj - 1, part], dkv_r.at[dj - 1, part], first + dj, first + dj, device
                ).start()
            if half == 0 and dj == 3:
                for place_at in (1, 2, 3):
                    arrived(dc1, S_DC2 + place_at)
                dc3[...] = (dc2[0] + dc2[1]) + (dc2[2] + dc2[3])
                dcf[z] = dc3[...]

                def taps_home(dz, _):
                    remote(dc3, dcf.at[z], S_DC3 + dz, S_DC3 + 8 - dz, near(dz, 0)).start()
                    return 0

                loop("taps_home", 1, 8, taps_home)
            if half == 1 and dj == 2:
                sum_blocks(0)

    for b in range(8):
        dq_s[b] = (dqa[:, b * 128 : b * 128 + 128] * 0.125).astype(BF16)
    z_rows = pl.ds(pl.multiple_of(z * 64, 64), 64)
    dq_o[z_rows, :] = dq_s[0]

    def dq_home(dz, _):
        remote(dq_s.at[dz], dq_o.at[z_rows], S_DQ + dz, S_DQ + 8 - dz, near(dz, 0)).start()
        return 0

    loop("dq_home", 1, 8, dq_home)

    sum_blocks(1)
    dkv_o[z] = dkv_z[0]

    def t_arrived(k, _):
        arrived(gr.at[k], S_T + k)
        return 0

    loop("t_arrived", 1, 32, t_arrived)
    tmp[...] = jnp.zeros((FR, 128), F32)
    for k in range(EXPERTS):
        tmp[k : k + 1, :] = gr[k]
    units = jnp.transpose(tmp[...]).astype(BF16)
    at = lax.broadcasted_iota(jnp.int32, (128, FR), 0)
    for r in range(2):
        line = dot(units, jnp.where(at == spot[r : r + 1, :], 1.0, 0.0).astype(BF16))
        own = at == (sid[r : r + 1, :] & 127)
        dgates_ref[r : r + 1, :] = jnp.sum(jnp.where(own, line, 0.0), axis=0, keepdims=True).astype(BF16)
    stores[5].start()

    def dq_arrived(k, _):
        arrived(dq_s.at[k], S_DQ + k)
        return 0

    loop("dq_arrived", 1, 8, dq_arrived)
    for n in range(4):
        cols = slice(n * 128, n * 128 + 128)
        dq_ref[:, cols] = jnp.transpose(dq_o[cols, :].astype(F32)).astype(BF16)
    stores[1].start()

    def dkv_arrived(k, _):
        arrived(dkv_z.at[k], S_DKVZ + k)
        return 0

    loop("dkv_arrived", 1, 8, dkv_arrived)
    for n in range(4):
        cols = slice(n * 128, n * 128 + 128)
        first = lanes_below((FR, 128), 64)
        one, two = dkv_o[2 * n].astype(F32), dkv_o[2 * n + 1].astype(F32)
        dk_ref[:, cols] = jnp.where(first, one, pltpu.roll(two, 64, 1)).astype(BF16)
        dv_ref[:, cols] = jnp.where(first, pltpu.roll(one, 64, 1), two).astype(BF16)
    stores[2].start()
    stores[3].start()

    def dc3_arrived(k, _):
        arrived(dc3, S_DC3 + k)
        return 0

    loop("dc3_arrived", 1, 8, dc3_arrived)
    for n in range(8):
        dconv_ref[:, n * 128 : n * 128 + 128] = dcf[n, 0:TAPS, :]
    stores[4].start()

    def rows_left(k, _):
        for first in (S_G, S_X, S_R):
            sent(sg.at[slot_rows(k)], first + k)
        sent(gr.at[k], S_T + k)
        return 0

    loop("rows_left", 1, 32, rows_left)

    def blocks_left(k, _):
        sent(qr.at[k], S_Q + k)
        sent(ks.at[k], S_KV + k)
        sent(dor.at[k], S_DO + k)
        sent(dkv_z.at[k], S_DKVZ + k)
        sent(dq_s.at[k], S_DQ + k)
        sent(dc_r.at[k], S_DC1 + k)
        sent(dc3, S_DC3 + k)
        return 0

    loop("blocks_left", 1, 8, blocks_left)
    for copy in halo_m_out + halo_g_out:
        copy.wait_send()
    for dj in (1, 2, 3):
        sent(kva.at[pl.ds(0, 1024)], S_KVP + dj)
        sent(dkv_s.at[dj - 1, pl.ds(0, 512)], S_DKVP + dj)
        sent(dkv_s.at[dj - 1, pl.ds(0, 512)], S_DKVP2 + dj)
        sent(dc1, S_DC2 + dj)
    for copy in stores:
        copy.wait()


def store(*refs):
    held, sems = refs[12:18], refs[18]
    ins = [pltpu.make_async_copy(refs[n], held[n], sems.at[n]) for n in range(6)]
    outs = [pltpu.make_async_copy(held[n], refs[6 + n], sems.at[6 + n]) for n in range(6)]
    for copy in ins:
        copy.start()
    for first, second in zip(ins, outs):
        first.wait()
        second.start()
    for copy in outs:
        copy.wait()


def on_device(*args):
    args = list(args)
    for n in (6, 9, 10, 11):
        args[n] = args[n].T
    anywhere = pl.BlockSpec(memory_space=pl.ANY)
    V = pltpu.VMEM
    scratch = [
        V((FR, D), BF16), V((FR, D), BF16), V((FR, 512), BF16), V((FR, 512), BF16), V((FR, 512), BF16), V((FR, 512), BF16),
        V((HEADS, FR), F32), V((TAPS, D), BF16), V((2, FR), F32), V((2, FR), jnp.int32), V((2, FR), jnp.int32),
        V((FR, D), BF16), V((FR, 512), BF16), V((FR, 512), BF16), V((FR, 512), BF16), V((TAPS, D), F32), V((2, FR), BF16),
        V((D, HID), BF16), V((HID, D), BF16), V((512, D), BF16),
        V((160, D), F32), V((160, D), F32), V((32, D), F32),
        V((2, 16, D), BF16), V((2, 16, D), BF16), V((FR, D), BF16), V((2, FR, ROWS), BF16),
        V((ROWS, D), BF16), V((ROWS, D), BF16), V((ROWS, D), BF16), V((ROWS, D), BF16),
        V((ROWS, HID), F32), V((FR, HID), BF16), V((ROWS, D), BF16), V((ROWS, D), BF16),
        V((4, 1, 128), F32), V((EXPERTS, 1, 128), F32),
        V((640, 128), BF16), V((8, 80, 128), BF16), V((8, FR, 128), BF16), V((KEYS, 128), BF16),
        V((128, 1024), BF16), V((1024, 128), BF16), V((1, 1024), F32), V((64, KEYS), BF16), V((KEYS, 1024), BF16),
        V((640, 128), BF16), V((8, 80, 128), BF16), V((128, 1024), BF16), V((1024, 128), BF16), V((1, 1024), F32),
        V((512, FR), F32), V((3, 1024, 128), BF16), V((3, 1024, 128), BF16),
        V((1024, 128), F32), V((8, FR, 128), BF16), V((8, FR, 128), BF16),
        V((64, 1024), F32), V((8, 64, 128), BF16), V((512, 128), BF16),
        V((8, 32, 128), F32), V((8, 32, 128), F32), V((32, 128), F32), V((4, 32, 128), F32), V((32, 128), F32),
        V((8, 32, 128), F32), V((FR, 128), F32), V((FR, 128), F32),
        V((1024, 128), F32),
        pltpu.SemaphoreType.DMA((SEMS,)), pltpu.SemaphoreType.DMA((SEMS,)), pltpu.SemaphoreType.DMA((3,)),
        pltpu.SemaphoreType.DMA((11,)), pltpu.SemaphoreType.DMA((6,)),
    ]
    shape = jax.ShapeDtypeStruct
    out_shape = (
        shape((FR, D), BF16), shape((FR, 512), BF16), shape((FR, 512), BF16), shape((FR, 512), BF16),
        shape((TAPS, D), F32), shape((2, FR), BF16),
    )
    found = pl.pallas_call(
        kernel,
        out_shape=out_shape,
        in_specs=[anywhere] * 14,
        out_specs=(anywhere,) * 6,
        scratch_shapes=scratch,
        compiler_params=pltpu.CompilerParams(
            collective_id=0, has_side_effects=True, vmem_limit_bytes=58 * 1024 * 1024
        ),
        name="conformer_backward",
    )(*args)
    results = pl.pallas_call(
        store,
        out_shape=out_shape,
        in_specs=[anywhere] * 6,
        out_specs=(anywhere,) * 6,
        scratch_shapes=[V(o.shape, o.dtype) for o in out_shape] + [pltpu.SemaphoreType.DMA((12,))],
        compiler_params=pltpu.CompilerParams(vmem_limit_bytes=60 * 1024 * 1024),
        name="store",
    )(*found)
    return (*results[:5], results[5].T)


def solution(mesh):
    frames = P(("grp", "ctx"), None)
    in_specs = (frames,) * 7 + (P(), P()) + (frames,) * 3 + (P("ctx", None, None),) * 2
    out_specs = (frames,) * 4 + (P("grp", None), frames)
    return jax.shard_map(on_device, mesh=mesh, in_specs=in_specs, out_specs=out_specs, check_vma=False)
```
